512 devices in a mesh: pool: 128 (over x, z, core), tp: 4 (over y).
Axes of the slice: x: 4, y: 4, z: 16, core: 2. Of those that a mesh axis runs over, the one named last changes fastest.
Arguments:
- queries: bfloat16 [1024, 16, 8192], P('pool', None, 'tp'), may hold values from -96 to 96
- self_key: bfloat16 [1024, 16, 1024], P('pool', None, 'tp'), may hold values from -4 to 4
- self_value: bfloat16 [1024, 16, 1024], P('pool', None, 'tp'), may hold values from -6 to 6
- passage_key: bfloat16 [512, 16, 1024], P('pool', None, 'tp'), may hold values from -6 to 6
- passage_value: bfloat16 [512, 16, 1024], P('pool', None, 'tp'), may hold values from -6 to 6
- out_grad: bfloat16 [1024, 16, 8192], P('pool', None, 'tp'), may hold values from -6 to 6
- block_ids: int32 [1024, 16], P('pool'), may hold values from 0 to 511, as said below
- block_valid: int32 [1024, 16], P('pool'), may hold values 0 or 1
- passage_slot: int32 [512], P(('pool', 'tp')), may hold values from 0 to 511, as said below
Outputs:
- query_grad: bfloat16 [1024, 16, 8192], P('pool', None, 'tp')
- self_key_grad: bfloat16 [1024, 16, 1024], P('pool', None, 'tp')
- self_value_grad: bfloat16 [1024, 16, 1024], P('pool', None, 'tp')
- passage_key_grad: bfloat16 [512, 16, 1024], P('pool', None, 'tp')
- passage_value_grad: bfloat16 [512, 16, 1024], P('pool', None, 'tp')
The draws below stay inside these ranges and needn't reach their ends.
Inputs may be any that keep to these rules, and one draw needn't show every extreme that they name: passage_slot is a permutation; the slots of one owner are the 4 consecutive ones that the pool index holds. `block_ids`: of the 128 entries of one pool index's lists, at most 2 name passages whose slots lie on one owner, and exactly 2 do for some owner.
All inputs are finite; a program needn't handle non-finite values. No bound on the sum of `block_valid` on one device may be relied on, other than what follows from the above.
Results may differ from the reference program's by a relative error of at most 0.04.
Values may be sent and summed in bfloat16 or wider, within the bound.
No kernel may reach another device: no remote copies, remote signals or barrier semaphores. Data moves between devices by JAX's collectives and lax.ppermute only.
A program may use at most 128 MiB of HBM per device.

```python
import jax
import jax.numpy as jnp
from jax import lax

HEADS = 64
KV_HEADS = 8
HD = 128
GROUP = 8
QLEN = 16
QPD = 8
NB = 16
LP = 16
P_DEV = 4
CAP = 2
QUERIES = 1024
PASSAGES = 512
N_POOL = 128


def routing(key):
    key_perm, key_pick = jax.random.split(key, 2)
    slot_of = jax.random.permutation(key_perm, PASSAGES).astype(jnp.int32)
    passage_at = jnp.argsort(slot_of).astype(jnp.int32)
    requests = QPD * NB
    spare = N_POOL * CAP - CAP
    need = requests - CAP

    def one_device(device_key):
        key_one, key_two, key_three, key_four, key_five = jax.random.split(device_key, 5)
        chosen = jnp.concatenate([jnp.arange(CAP, dtype=jnp.int32), CAP + jax.random.permutation(key_one, spare)[:need].astype(jnp.int32)])
        offset = jax.random.randint(key_two, (), 0, N_POOL)
        owner = (chosen // CAP + offset) % N_POOL
        local = jnp.minimum(jax.random.randint(key_three, (requests,), 0, P_DEV), jax.random.randint(key_four, (requests,), 0, P_DEV))
        order = jax.random.permutation(key_five, requests)
        return passage_at[(owner * P_DEV + local)[order]]
    ids = jax.vmap(one_device)(jax.random.split(key_pick, N_POOL))
    return (slot_of, ids.reshape(QUERIES, NB).astype(jnp.int32))


def attention_inputs(key):
    key_k, key_q = jax.random.split(key, 2)
    keys = jnp.clip(jax.random.normal(key_k, (QUERIES, QLEN, KV_HEADS, HD), jnp.float32), -4.0, 4.0)
    queries = jnp.clip(jax.random.normal(key_q, (QUERIES, QLEN, KV_HEADS, GROUP, HD), jnp.float32), -4.0, 4.0)
    return (queries.reshape(QUERIES, QLEN, HEADS * HD), keys.reshape(QUERIES, QLEN, KV_HEADS * HD))


def draw_passage_slot(key, part):
    return routing(key)[0]


def draw_block_ids(key, part):
    return routing(key)[1]


def draw_queries(key, part):
    return attention_inputs(key)[0].astype(jnp.bfloat16)


def draw_self_key(key, part):
    return attention_inputs(key)[1].astype(jnp.bfloat16)


def set_ends(entries, rng, smallest, largest):
    longest = entries.shape.index(max(entries.shape))
    spots = []
    for shift in (0, 1):
        where = [jax.random.randint(jax.random.fold_in(rng, axis), (), 0, length) for axis, length in enumerate(entries.shape)]
        where[longest] = (where[longest] + shift) % entries.shape[longest]
        spots.append(tuple(where))
    return entries.at[spots[0]].set(smallest).at[spots[1]].set(largest)


def steps_of(rng, extent, cuts, smallest, top_value):
    factor_of = 1.0
    for position, shards_of in cuts:
        steps = jax.random.uniform(jax.random.fold_in(jax.random.fold_in(rng, 6), position), (shards_of,), jnp.float32, smallest / len(cuts), top_value / len(cuts))
        factor_of = factor_of * jnp.repeat(jnp.exp(steps), extent[position] // shards_of).reshape((-1,) + (1,) * (len(extent) - 1 - position))
    return factor_of


def noise(stream_key, shape, scale, reach, pieces=(), held_as=jnp.bfloat16):
    loudness = steps_of(stream_key, shape, pieces, -0.22, 0.18) if pieces else 1.0
    values = jax.random.normal(stream_key, shape, jnp.float32) * scale * loudness
    return jnp.minimum(jnp.maximum(values, -reach), reach).astype(held_as)


def setup_inputs(seed: int = 0) -> dict:
    arg_keys = jax.random.split(jax.random.key(seed), 10)
    queries = draw_queries(jax.random.fold_in(arg_keys[9], 71), 0)
    self_key = draw_self_key(jax.random.fold_in(arg_keys[9], 71), 0)
    self_value = noise(arg_keys[2], (QUERIES, QLEN, KV_HEADS * HD), 1.0, 6.0, ((0, 128), (2, 4)))
    passage_key = noise(arg_keys[3], (PASSAGES, LP, KV_HEADS * HD), 1.0, 6.0, ((0, 128), (2, 4)))
    passage_value = noise(arg_keys[4], (PASSAGES, LP, KV_HEADS * HD), 1.0, 6.0, ((0, 128), (2, 4)))
    out_grad = noise(arg_keys[5], (QUERIES, QLEN, HEADS * HD), 1.0, 6.0, ((0, 128), (2, 4)))
    block_ids = draw_block_ids(jax.random.fold_in(arg_keys[9], 71), 0)
    block_valid = set_ends((jax.random.randint(arg_keys[7], (QUERIES, NB), 0, 4) < 3).astype(jnp.int32), jax.random.fold_in(arg_keys[7], 1), 0, 1)
    passage_slot = draw_passage_slot(jax.random.fold_in(arg_keys[9], 71), 0)
    return {"queries": queries, "self_key": self_key, "self_value": self_value, "passage_key": passage_key, "passage_value": passage_value, "out_grad": out_grad, "block_ids": block_ids, "block_valid": block_valid, "passage_slot": passage_slot}


def backward(q, keys, values, dout, allowed):
    qlen = q.shape[0]
    span = keys.shape[0]
    kvh = keys.shape[1] // HD
    group = q.shape[1] // (kvh * HD)
    scale = HD ** -0.5
    qg = q.reshape(qlen, kvh, group, HD).astype(jnp.float32)
    kg = keys.reshape(span, kvh, HD).astype(jnp.float32)
    vg = values.reshape(span, kvh, HD).astype(jnp.float32)
    dg = dout.reshape(qlen, kvh, group, HD).astype(jnp.float32)
    scores = jnp.einsum("lkgd,skd->kgls", qg, kg) * scale
    scores = jnp.where(allowed, scores, -1e30)
    top = jnp.max(scores, axis=-1, keepdims=True)
    weights = jnp.where(allowed, jnp.exp(scores - top), 0.0)
    probs = weights / jnp.sum(weights, axis=-1, keepdims=True)
    probs_low = probs.astype(jnp.bfloat16)
    out_low = jnp.einsum("kgls,skd->lkgd", probs_low.astype(jnp.float32), vg).astype(jnp.bfloat16)
    delta = jnp.einsum("lkgd,lkgd->kgl", dg, out_low.astype(jnp.float32))
    dprob = jnp.einsum("lkgd,skd->kgls", dg, vg)
    dscore = (probs * (dprob - delta[..., None])).astype(jnp.bfloat16).astype(jnp.float32)
    query_grad = (jnp.einsum("kgls,skd->lkgd", dscore, kg) * scale).astype(jnp.bfloat16).reshape(qlen, -1)
    key_part = (jnp.einsum("kgls,lkgd->skd", dscore, qg) * scale).reshape(span, -1)
    value_part = jnp.einsum("kgls,lkgd->skd", probs_low.astype(jnp.float32), dg).reshape(span, -1)
    return query_grad, key_part, value_part


def lowered(values):
    return lax.optimization_barrier(values.astype(jnp.bfloat16)).astype(jnp.float32)


def reference(queries, self_key, self_value, passage_key, passage_value, out_grad, block_ids, block_valid, passage_slot):
    slots = passage_slot[block_ids].astype(jnp.int32)
    feat = passage_key.shape[2]
    zero = jnp.zeros((PASSAGES, LP, feat), jnp.float32)
    causal = jnp.arange(QLEN)[None, :] <= jnp.arange(QLEN)[:, None]
    width = NB * LP

    def step(carry, item):
        grad_key, grad_value = carry
        q, own_key, own_value, dout, slot_list, valid = item
        keys = jnp.concatenate([passage_key[slot_list].reshape(width, feat), own_key], axis=0)
        values = jnp.concatenate([passage_value[slot_list].reshape(width, feat), own_value], axis=0)
        passage_ok = jnp.broadcast_to((valid > 0)[:, None], (NB, LP)).reshape(1, width)
        allowed = jnp.concatenate([jnp.broadcast_to(passage_ok, (QLEN, width)), causal], axis=1)
        query_grad, key_part, value_part = backward(q, keys, values, dout, allowed)
        grad_key = grad_key.at[slot_list].add(lowered(key_part[:width]).reshape(NB, LP, feat))
        grad_value = grad_value.at[slot_list].add(lowered(value_part[:width]).reshape(NB, LP, feat))
        return (grad_key, grad_value), (query_grad, key_part[width:].astype(jnp.bfloat16), value_part[width:].astype(jnp.bfloat16))

    (grad_key, grad_value), (query_grad, self_key_grad, self_value_grad) = lax.scan(
        step, (zero, zero), (queries, self_key, self_value, out_grad, slots, block_valid))
    return query_grad, self_key_grad, self_value_grad, grad_key.astype(jnp.bfloat16), grad_value.astype(jnp.bfloat16)
```

```python
import jax
import jax.numpy as jnp
from jax import lax
from jax.experimental import pallas as pl
from jax.experimental.pallas import tpu as pltpu
from jax.sharding import Mesh
from jax.sharding import PartitionSpec as P

HD = 128
GROUP = 8
QLEN = 16
LP = 16
NB = 16
QPD = 8
P_DEV = 4
CHIP_P = 2 * P_DEV
XS, ZH, ZL = 4, 4, 4
ZS = ZH * ZL
TILES = 2 * CHIP_P
ROWS = TILES + 1
COLUMN = ZS * ROWS
GCOLUMN = ZS * TILES
SCALE = HD ** (-0.5)
SPAN = NB * LP
WIDE = 2 * GROUP * HD + 2 * HD
BF = jnp.bfloat16
F32 = jnp.float32


def ring(n, d):
    return [(i, (i + d) % n) for i in range(n)]


def dot(a, b, ca, cb):
    return lax.dot_general(a, b, (((ca,), (cb,)), ((), ())), preferred_element_type=F32)


def attention_kernel(
    where_ref,
    gwhere_ref,
    valid_ref,
    s0,
    s1,
    s2a,
    s2b,
    s3,
    mine,
    other,
    g0,
    g1,
    g2a,
    g2b,
    g3,
    dq_mine,
    dq_other,
    self_mine,
    self_other,
    store,
    grads,
    sem_in,
    sem_out,
):
    half = COLUMN // 2
    loads = [
        pltpu.make_async_copy(src, store.at[pl.ds(start, size)], sem_in.at[i])
        for i, (src, start, size) in enumerate(
            [
                (s0, 0, COLUMN),
                (s1, COLUMN, COLUMN),
                (s2a, 2 * COLUMN, half),
                (s2b, 2 * COLUMN + half, half),
                (s3, 3 * COLUMN, COLUMN),
            ]
        )
    ]
    for copy in loads:
        copy.start()

    def clear(i, carry):
        grads[pl.ds(i * 16, 16)] = jnp.zeros((16, LP, HD), BF)
        return carry

    lax.fori_loop(0, XS * GCOLUMN // 16, clear, 0)
    for copy in loads:
        copy.wait()

    u = lax.broadcasted_iota(jnp.int32, (QLEN, GROUP * QLEN), 0)
    t = lax.broadcasted_iota(jnp.int32, (QLEN, GROUP * QLEN), 1) % QLEN
    causal = jnp.where(u <= t, 0.0, -1e30).astype(F32)

    def stacked(ref, b, start):
        return jnp.concatenate(
            [ref[b, :, start + g * HD : start + (g + 1) * HD] for g in range(GROUP)], axis=0
        )

    def one(b, base, pack, dq_out, self_out):
        row = (base + b) * NB
        at = [where_ref[row + j] for j in range(NB)]
        q = stacked(pack, b, 0)
        do = stacked(pack, b, GROUP * HD)
        own = 2 * GROUP * HD
        keys = jnp.concatenate([store[i] for i in at] + [pack[b, :, own : own + HD]], axis=0)
        values = jnp.concatenate(
            [store[i + 1] for i in at] + [pack[b, :, own + HD : own + 2 * HD]], axis=0
        )
        bias = jnp.concatenate(
            [
                jnp.full((LP, GROUP * QLEN), jnp.where(valid_ref[row + j] > 0, 0.0, -1e30), F32)
                for j in range(NB)
            ]
            + [causal],
            axis=0,
        )
        scores = dot(keys, q, 1, 1) * SCALE + bias
        top = jnp.max(scores, axis=0, keepdims=True)
        weights = jnp.exp(scores - top)
        probs = weights * (1.0 / jnp.sum(weights, axis=0, keepdims=True))
        low = probs.astype(BF)
        dprob = dot(values, do, 1, 1)
        delta = jnp.sum(probs * dprob, axis=0, keepdims=True)
        dscore = (probs * (dprob - delta)).astype(BF)
        dq = (dot(dscore, keys, 0, 0) * SCALE).astype(BF)
        for g in range(GROUP):
            dq_out[b, :, g * HD : (g + 1) * HD] = dq[g * QLEN : (g + 1) * QLEN]
        dk = (dot(dscore, q, 1, 0) * SCALE).astype(BF)
        dv = dot(low, do, 1, 0).astype(BF)
        self_out[b, :, :HD] = dk[SPAN:]
        self_out[b, :, HD:] = dv[SPAN:]
        for j in range(NB):
            to = gwhere_ref[row + j]
            for k, part in enumerate((dk, dv)):
                grads[to + k] = (
                    grads[to + k].astype(F32) + part[j * LP : (j + 1) * LP].astype(F32)
                ).astype(BF)

    def step(b, carry):
        one(b, 0, mine, dq_mine, self_mine)
        one(b, QPD, other, dq_other, self_other)
        return carry

    lax.fori_loop(0, QPD, step, 0)
    ghalf = GCOLUMN // 2
    stores = [
        pltpu.make_async_copy(grads.at[pl.ds(start, size)], dst, sem_out.at[i])
        for i, (dst, start, size) in enumerate(
            [
                (g2a, 2 * GCOLUMN, ghalf),
                (g2b, 2 * GCOLUMN + ghalf, ghalf),
                (g1, GCOLUMN, GCOLUMN),
                (g3, 3 * GCOLUMN, GCOLUMN),
                (g0, 0, GCOLUMN),
            ]
        )
    ]
    for copy in stores:
        copy.start()
    for copy in stores:
        copy.wait()


def attention(where, gwhere, valid, s0, s1, s2a, s2b, s3, mine, other):
    smem = pl.BlockSpec(memory_space=pltpu.SMEM)
    vmem = pl.BlockSpec(memory_space=pltpu.VMEM)
    hbm = pl.BlockSpec(memory_space=pl.ANY)

    def tiles(n):
        return jax.ShapeDtypeStruct((n, LP, HD), BF)

    query = jax.ShapeDtypeStruct((QPD, QLEN, GROUP * HD), BF)
    own = jax.ShapeDtypeStruct((QPD, QLEN, 2 * HD), BF)
    return pl.pallas_call(
        attention_kernel,
        out_shape=(
            tiles(GCOLUMN),
            tiles(GCOLUMN),
            tiles(GCOLUMN // 2),
            tiles(GCOLUMN // 2),
            tiles(GCOLUMN),
            query,
            query,
            own,
            own,
        ),
        in_specs=[smem] * 3 + [hbm] * 5 + [vmem] * 2,
        out_specs=(hbm,) * 5 + (vmem,) * 4,
        scratch_shapes=[
            pltpu.VMEM((XS * COLUMN, LP, HD), BF),
            pltpu.VMEM((XS * GCOLUMN, LP, HD), BF),
            pltpu.SemaphoreType.DMA((5,)),
            pltpu.SemaphoreType.DMA((5,)),
        ],
        compiler_params=pltpu.CompilerParams(vmem_limit_bytes=40 * 2**20),
        cost_estimate=pl.CostEstimate(
            flops=16 * 5 * 2 * 272 * 128 * 128, bytes_accessed=12 * 2**20, transcendentals=16 * 272 * 128
        ),
    )(where, gwhere, valid, s0, s1, s2a, s2b, s3, mine, other)


def total(*parts):
    out = parts[0].astype(F32)
    for part in parts[1:]:
        out = out + part.astype(F32)
    return out.astype(BF)


def per_device(
    queries,
    self_key,
    self_value,
    passage_key,
    passage_value,
    out_grad,
    block_ids,
    block_valid,
    passage_slot,
):
    core = lax.axis_index("core")
    my_x = lax.axis_index("x")
    swap = ring(2, 1)
    feat = GROUP * HD

    def head(array, c, width):
        return lax.dynamic_slice_in_dim(array, c * width, width, axis=array.ndim - 1)

    def passages(c):
        return jnp.stack([head(passage_key, c, HD), head(passage_value, c, HD)], axis=1)

    def by_core(mine_part, other_part, axis):
        first = jnp.where(core == 0, mine_part, other_part)
        second = jnp.where(core == 0, other_part, mine_part)
        return jnp.concatenate([first, second], axis=axis)

    chip_slots = lax.all_to_all(
        jnp.broadcast_to(passage_slot, (8,)), ("core", "tp"), split_axis=0, concat_axis=0, tiled=True
    )
    kv_other = lax.ppermute(passages(1 - core), "core", swap)
    kv_chip = by_core(passages(core), kv_other, 0).reshape(TILES, LP, HD)
    coded = jnp.concatenate([chip_slots // 16, chip_slots % 16]).astype(BF)
    code_tile = jnp.pad(coded.reshape(1, 1, 16), ((0, 0), (0, LP - 1), (0, HD - 16)))
    payload = jnp.concatenate([kv_chip, code_tile], axis=0)

    def pack(c):
        return jnp.concatenate(
            [
                head(queries, c, feat),
                head(out_grad, c, feat),
                head(self_key, c, HD),
                head(self_value, c, HD),
            ],
            axis=2,
        )

    mine = pack(core)
    other = lax.ppermute(pack(1 - core), "core", swap)
    lists = jnp.stack([block_ids, block_valid])
    lists_other = lax.ppermute(lists, "core", swap)

    far = lax.all_to_all(
        jnp.broadcast_to(payload[None], (ZH, ROWS, LP, HD)), "zh", split_axis=0, concat_axis=0, tiled=True
    )
    near = lax.all_to_all(
        jnp.broadcast_to(far[None], (ZL, ZH, ROWS, LP, HD)), "zl", split_axis=0, concat_axis=0, tiled=True
    )
    s0 = near.reshape(COLUMN, LP, HD)
    half = COLUMN // 2
    s1 = lax.ppermute(s0, "x", ring(XS, -1))
    s3 = lax.ppermute(s0, "x", ring(XS, 1))
    s2a = lax.ppermute(s1[:half], "x", ring(XS, -1))
    s2b = lax.ppermute(s3[half:], "x", ring(XS, 1))

    def place(number):
        pool = number // P_DEV
        x = pool // (2 * ZS)
        z = pool // 2 % ZS
        dx = (x - my_x) % XS
        return dx * ZS + z % ZL * ZH + z // ZL, pool % 2 * P_DEV + number % P_DEV

    codes = jnp.concatenate(
        [s.reshape(-1, ROWS, LP, HD)[:, TILES, 0, :16] for s in (s0, s1, s2a, s2b, s3)], axis=0
    ).astype(jnp.int32)
    slot_of = (codes[:, :CHIP_P] * 16 + codes[:, CHIP_P:]).reshape(-1)
    ids = jnp.concatenate([block_ids, lists_other[0]]).reshape(-1)
    valid = jnp.concatenate([block_valid, lists_other[1]]).reshape(-1)
    chip, inner = place(ids)
    id_at = chip * CHIP_P + inner
    every = jnp.arange(slot_of.shape[0], dtype=jnp.int32)
    slots = jnp.sum(jnp.where(id_at[:, None] == every[None, :], slot_of[None, :], 0), axis=1)
    chip, inner = place(slots)
    where = chip * ROWS + 2 * inner
    gwhere = chip * TILES + 2 * inner

    g0, g1, g2a, g2b, g3, dq_mine, dq_other, self_mine, self_other = attention(
        where, gwhere, valid, s0, s1, s2a, s2b, s3, mine, other
    )

    ghalf = GCOLUMN // 2
    via_a = lax.ppermute(g2a, "x", ring(XS, 1))
    via_b = lax.ppermute(g2b, "x", ring(XS, -1))
    up = jnp.concatenate([total(g1[:ghalf], via_a), g1[ghalf:]], axis=0)
    down = jnp.concatenate([g3[:ghalf], total(g3[ghalf:], via_b)], axis=0)
    from_below = lax.ppermute(up, "x", ring(XS, 1))
    from_above = lax.ppermute(down, "x", ring(XS, -1))
    column = total(g0, from_below, from_above).reshape(ZL, ZH, TILES, LP, HD)
    near_parts = lax.all_to_all(column, "zl", split_axis=0, concat_axis=0, tiled=True)
    near_sum = total(*[near_parts[i] for i in range(ZL)])
    far_parts = lax.all_to_all(near_sum, "zh", split_axis=0, concat_axis=0, tiled=True)
    chip_sum = total(*[far_parts[i] for i in range(ZH)]).reshape(2, P_DEV, 2, LP, HD)
    kept = lax.dynamic_index_in_dim(chip_sum, core, 0, keepdims=False)
    given = lax.dynamic_index_in_dim(chip_sum, 1 - core, 0, keepdims=False)
    taken = lax.ppermute(given, "core", swap)
    grad = by_core(kept, taken, 3)

    dq_taken = lax.ppermute(dq_other, "core", swap)
    self_taken = lax.ppermute(self_other, "core", swap)
    query_grad = by_core(dq_mine, dq_taken, 2)
    self_key_grad = by_core(self_mine[:, :, :HD], self_taken[:, :, :HD], 2)
    self_value_grad = by_core(self_mine[:, :, HD:], self_taken[:, :, HD:], 2)
    return (query_grad, self_key_grad, self_value_grad, grad[:, 0], grad[:, 1])


def solution(mesh):
    fine = Mesh(mesh.devices.reshape(XS, ZH, ZL, 2, 4), ("x", "zh", "zl", "core", "tp"))
    pool = ("x", "zh", "zl", "core")
    rows = P(pool, None, "tp")
    return jax.shard_map(
        per_device,
        mesh=fine,
        in_specs=(rows,) * 6 + (P(pool, None), P(pool, None), P(pool + ("tp",))),
        out_specs=(rows,) * 5,
        check_vma=False,
    )
```

```python
import jax
import jax.numpy as jnp
from jax import lax
from jax.experimental import pallas as pl
from jax.experimental.pallas import tpu as pltpu
from jax.sharding import Mesh
from jax.sharding import PartitionSpec as P

HD = 128
GROUP = 8
QLEN = 16
LP = 16
NB = 16
QPD = 8
P_DEV = 4
XS, ZH, ZL, TP = 4, 4, 4, 4
ZS = ZH * ZL
TILES = 2 * P_DEV
CLASS = XS * ZH * 2 * TILES
SCALE = HD ** (-0.5)
SPAN = NB * LP
WIDE = 2 * GROUP * HD + 2 * HD
BF = jnp.bfloat16
F32 = jnp.float32


def ring(n, d):
    return [(i, (i + d) % n) for i in range(n)]


def dot(a, b, ca, cb):
    return lax.dot_general(a, b, (((ca,), (cb,)), ((), ())), preferred_element_type=F32)


def attention_kernel(
    where_ref,
    valid_ref,
    s0,
    s1,
    s2a,
    s2b,
    s3,
    mine,
    other,
    g0,
    g1,
    g2a,
    g2b,
    g3,
    dq_mine,
    dq_other,
    self_mine,
    self_other,
    store,
    grads,
    sem_in,
    sem_out,
):
    half = CLASS // 2
    loads = [
        pltpu.make_async_copy(src, store.at[pl.ds(start, size)], sem_in.at[i])
        for i, (src, start, size) in enumerate(
            [
                (s0, 0, CLASS),
                (s1, CLASS, CLASS),
                (s2a, 2 * CLASS, half),
                (s2b, 2 * CLASS + half, half),
                (s3, 3 * CLASS, CLASS),
            ]
        )
    ]
    for copy in loads:
        copy.start()

    def clear(i, carry):
        grads[pl.ds(i * 16, 16)] = jnp.zeros((16, LP, HD), BF)
        return carry

    lax.fori_loop(0, ZL * CLASS // 16, clear, 0)
    for copy in loads:
        copy.wait()

    u = lax.broadcasted_iota(jnp.int32, (QLEN, GROUP * QLEN), 0)
    t = lax.broadcasted_iota(jnp.int32, (QLEN, GROUP * QLEN), 1) % QLEN
    causal = jnp.where(u <= t, 0.0, -1e30).astype(F32)

    def stacked(ref, b, start):
        return jnp.concatenate(
            [ref[b, :, start + g * HD : start + (g + 1) * HD] for g in range(GROUP)], axis=0
        )

    def one(b, base, pack, dq_out, self_out):
        row = (base + b) * NB
        at = [where_ref[row + j] for j in range(NB)]
        q = stacked(pack, b, 0)
        do = stacked(pack, b, GROUP * HD)
        own = 2 * GROUP * HD
        keys = jnp.concatenate([store[i] for i in at] + [pack[b, :, own : own + HD]], axis=0)
        values = jnp.concatenate(
            [store[i + 1] for i in at] + [pack[b, :, own + HD : own + 2 * HD]], axis=0
        )
        bias = jnp.concatenate(
            [
                jnp.full((LP, GROUP * QLEN), jnp.where(valid_ref[row + j] > 0, 0.0, -1e30), F32)
                for j in range(NB)
            ]
            + [causal],
            axis=0,
        )
        scores = dot(keys, q, 1, 1) * SCALE + bias
        top = jnp.max(scores, axis=0, keepdims=True)
        weights = jnp.exp(scores - top)
        probs = weights * (1.0 / jnp.sum(weights, axis=0, keepdims=True))
        low = probs.astype(BF)
        dprob = dot(values, do, 1, 1)
        delta = jnp.sum(probs * dprob, axis=0, keepdims=True)
        dscore = (probs * (dprob - delta)).astype(BF)
        dq = (dot(dscore, keys, 0, 0) * SCALE).astype(BF)
        for g in range(GROUP):
            dq_out[b, :, g * HD : (g + 1) * HD] = dq[g * QLEN : (g + 1) * QLEN]
        dk = (dot(dscore, q, 1, 0) * SCALE).astype(BF)
        dv = dot(low, do, 1, 0).astype(BF)
        self_out[b, :, :HD] = dk[SPAN:]
        self_out[b, :, HD:] = dv[SPAN:]
        for j in range(NB):
            for k, part in enumerate((dk, dv)):
                to = at[j] + k
                grads[to] = (
                    grads[to].astype(F32) + part[j * LP : (j + 1) * LP].astype(F32)
                ).astype(BF)

    def step(b, carry):
        one(b, 0, mine, dq_mine, self_mine)
        one(b, QPD, other, dq_other, self_other)
        return carry

    lax.fori_loop(0, QPD, step, 0)
    stores = [
        pltpu.make_async_copy(grads.at[pl.ds(start, size)], dst, sem_out.at[i])
        for i, (dst, start, size) in enumerate(
            [
                (g2a, 2 * CLASS, half),
                (g2b, 2 * CLASS + half, half),
                (g1, CLASS, CLASS),
                (g3, 3 * CLASS, CLASS),
                (g0, 0, CLASS),
            ]
        )
    ]
    for copy in stores:
        copy.start()
    for copy in stores:
        copy.wait()


def attention(where, valid, s0, s1, s2a, s2b, s3, mine, other):
    smem = pl.BlockSpec(memory_space=pltpu.SMEM)
    vmem = pl.BlockSpec(memory_space=pltpu.VMEM)
    hbm = pl.BlockSpec(memory_space=pl.ANY)

    def tiles(n):
        return jax.ShapeDtypeStruct((n, LP, HD), BF)

    query = jax.ShapeDtypeStruct((QPD, QLEN, GROUP * HD), BF)
    own = jax.ShapeDtypeStruct((QPD, QLEN, 2 * HD), BF)
    return pl.pallas_call(
        attention_kernel,
        out_shape=(
            tiles(CLASS),
            tiles(CLASS),
            tiles(CLASS // 2),
            tiles(CLASS // 2),
            tiles(CLASS),
            query,
            query,
            own,
            own,
        ),
        in_specs=[smem] * 2 + [hbm] * 5 + [vmem] * 2,
        out_specs=(hbm,) * 5 + (vmem,) * 4,
        scratch_shapes=[
            pltpu.VMEM((ZL * CLASS, LP, HD), BF),
            pltpu.VMEM((ZL * CLASS, LP, HD), BF),
            pltpu.SemaphoreType.DMA((5,)),
            pltpu.SemaphoreType.DMA((5,)),
        ],
        compiler_params=pltpu.CompilerParams(vmem_limit_bytes=40 * 2**20),
        cost_estimate=pl.CostEstimate(
            flops=16 * 5 * 2 * 272 * 128 * 128, bytes_accessed=12 * 2**20, transcendentals=16 * 272 * 128
        ),
    )(where, valid, s0, s1, s2a, s2b, s3, mine, other)


def total(*parts):
    out = parts[0].astype(F32)
    for part in parts[1:]:
        out = out + part.astype(F32)
    return out.astype(BF)


def per_device(
    queries,
    self_key,
    self_value,
    passage_key,
    passage_value,
    out_grad,
    block_ids,
    block_valid,
    passage_slot,
):
    core = lax.axis_index("core")
    my_zl = lax.axis_index("zl")
    swap = ring(2, 1)
    around = ("zh", "zl")
    feat = GROUP * HD
    half = CLASS // 2

    def head(array, c, width):
        return lax.dynamic_slice_in_dim(array, c * width, width, axis=array.ndim - 1)

    def by_core(mine_part, other_part, axis):
        first = jnp.where(core == 0, mine_part, other_part)
        second = jnp.where(core == 0, other_part, mine_part)
        return jnp.concatenate([first, second], axis=axis)

    code = jnp.concatenate([passage_slot // 16, passage_slot % 16]).astype(BF)
    code_tile = jnp.pad(code.reshape(1, 1, 2), ((0, 0), (0, LP - 1), (0, HD - 2)))

    def passages(c):
        lanes = slice(c * HD, (c + 1) * HD)
        both = jnp.stack([passage_key[:, :, lanes], passage_value[:, :, lanes]], axis=1)
        return jnp.concatenate([both.reshape(TILES, LP, HD), code_tile], axis=0)

    heads = jnp.stack([passages(0), passages(1)])
    far = lax.all_to_all(
        jnp.broadcast_to(heads[None], (ZH, 2, TILES + 1, LP, HD)).reshape(2 * ZH, TILES + 1, LP, HD),
        ("zh", "core"),
        split_axis=0,
        concat_axis=0,
        tiled=True,
    )
    s0 = lax.all_to_all(
        jnp.broadcast_to(far[None, :, :TILES], (XS, 2 * ZH, TILES, LP, HD)),
        "x",
        split_axis=0,
        concat_axis=0,
        tiled=True,
    ).reshape(CLASS, LP, HD)
    s1 = lax.ppermute(s0, around, ring(ZS, -1))
    s3 = lax.ppermute(s0, around, ring(ZS, 1))
    s2a = lax.ppermute(s1[:half], around, ring(ZS, -1))
    s2b = lax.ppermute(s3[half:], around, ring(ZS, 1))

    def pack(c):
        return jnp.concatenate(
            [
                head(queries, c, feat),
                head(out_grad, c, feat),
                head(self_key, c, HD),
                head(self_value, c, HD),
            ],
            axis=2,
        )

    mine = pack(core)
    other = lax.ppermute(pack(1 - core), "core", swap)
    lists = jnp.stack([block_ids, block_valid])
    lists_other = lax.ppermute(lists, "core", swap)

    codes = far[:, TILES, 0, :2].astype(jnp.int32)
    known = codes[:, 0] * 16 + codes[:, 1]
    known, _ = lax.optimization_barrier((known, s0[:1, 0, :1]))
    slot_of = lax.all_to_all(
        jnp.broadcast_to(known[None], (XS * ZL * TP, 2 * ZH)),
        ("x", "zl", "tp"),
        split_axis=0,
        concat_axis=0,
        tiled=True,
    ).reshape(-1)

    def parts(number):
        pool = number // P_DEV
        z = pool // 2 % ZS
        return pool // (2 * ZS), z // ZL, z % ZL, pool % 2, number % P_DEV

    ids = jnp.concatenate([block_ids, lists_other[0]]).reshape(-1)
    valid = jnp.concatenate([block_valid, lists_other[1]]).reshape(-1)
    x, zh, zl, c, inner = parts(ids)
    id_at = (((x * ZL + zl) * TP + inner) * ZH + zh) * 2 + c
    every = jnp.arange(slot_of.shape[0], dtype=jnp.int32)
    slots = jnp.sum(jnp.where(id_at[:, None] == every[None, :], slot_of[None, :], 0), axis=1)
    x, zh, zl, c, inner = parts(slots)
    where = ((((zl - my_zl) % ZL * XS + x) * ZH + zh) * 2 + c) * TILES + 2 * inner

    g0, g1, g2a, g2b, g3, dq_mine, dq_other, self_mine, self_other = attention(
        where, valid, s0, s1, s2a, s2b, s3, mine, other
    )

    via_a = lax.ppermute(g2a, around, ring(ZS, 1))
    via_b = lax.ppermute(g2b, around, ring(ZS, -1))
    up = jnp.concatenate([total(g1[:half], via_a), g1[half:]], axis=0)
    down = jnp.concatenate([g3[:half], total(g3[half:], via_b)], axis=0)
    from_below = lax.ppermute(up, around, ring(ZS, 1))
    from_above = lax.ppermute(down, around, ring(ZS, -1))
    summed = total(g0, from_below, from_above).reshape(XS, 2 * ZH, TILES, LP, HD)
    x_parts = lax.all_to_all(summed, "x", split_axis=0, concat_axis=0, tiled=True)
    x_sum = total(*[x_parts[i] for i in range(XS)])
    far_parts = lax.all_to_all(x_sum, ("zh", "core"), split_axis=0, concat_axis=0, tiled=True)
    far_parts = far_parts.reshape(ZH, 2, P_DEV, 2, LP, HD)
    grad = total(*[far_parts[i] for i in range(ZH)])
    key_grad = jnp.concatenate([grad[0, :, 0], grad[1, :, 0]], axis=2)
    value_grad = jnp.concatenate([grad[0, :, 1], grad[1, :, 1]], axis=2)

    dq_taken = lax.ppermute(dq_other, "core", swap)
    self_taken = lax.ppermute(self_other, "core", swap)
    query_grad = by_core(dq_mine, dq_taken, 2)
    self_key_grad = by_core(self_mine[:, :, :HD], self_taken[:, :, :HD], 2)
    self_value_grad = by_core(self_mine[:, :, HD:], self_taken[:, :, HD:], 2)
    return (query_grad, self_key_grad, self_value_grad, key_grad, value_grad)


def solution(mesh):
    fine = Mesh(mesh.devices.reshape(XS, ZH, ZL, 2, TP), ("x", "zh", "zl", "core", "tp"))
    pool = ("x", "zh", "zl", "core")
    rows = P(pool, None, "tp")
    return jax.shard_map(
        per_device,
        mesh=fine,
        in_specs=(rows,) * 6 + (P(pool, None), P(pool, None), P(pool + ("tp",))),
        out_specs=(rows,) * 5,
        check_vma=False,
    )
```

```python
import jax
import jax.numpy as jnp
from jax import lax
from jax.experimental import pallas as pl
from jax.experimental.pallas import tpu as pltpu
from jax.sharding import Mesh
from jax.sharding import PartitionSpec as P

HD = 128
GROUP = 8
QLEN = 16
LP = 16
NB = 16
QPD = 8
P_DEV = 4
XS, ZH, ZL, TP = 4, 4, 4, 4
ZS = ZH * ZL
TILES = 2 * P_DEV
HALF = XS * ZH * TILES
PARTS = 2 * ZL
SCALE = HD ** (-0.5)
SPAN = NB * LP
BF = jnp.bfloat16
F32 = jnp.float32


def ring(n, d):
    return [(i, (i + d) % n) for i in range(n)]


def dot(a, b, ca, cb):
    return lax.dot_general(a, b, (((ca,), (cb,)), ((), ())), preferred_element_type=F32)


def attention_kernel(
    where_ref,
    valid_ref,
    *refs,
):
    stored, (mine, other) = refs[:PARTS], refs[PARTS : PARTS + 2]
    outs = refs[PARTS + 2 : 2 * PARTS + 2]
    dq_mine, dq_other, self_mine, self_other = refs[2 * PARTS + 2 : 2 * PARTS + 6]
    store, grads, sem_in, sem_out = refs[2 * PARTS + 6 :]
    loads = [
        pltpu.make_async_copy(src, store.at[pl.ds(i * HALF, HALF)], sem_in.at[i])
        for i, src in enumerate(stored)
    ]
    for copy in loads:
        copy.start()

    def clear(i, carry):
        grads[pl.ds(i * 16, 16)] = jnp.zeros((16, LP, HD), BF)
        return carry

    lax.fori_loop(0, PARTS * HALF // 16, clear, 0)
    for copy in loads:
        copy.wait()

    u = lax.broadcasted_iota(jnp.int32, (QLEN, GROUP * QLEN), 0)
    t = lax.broadcasted_iota(jnp.int32, (QLEN, GROUP * QLEN), 1) % QLEN
    causal = jnp.where(u <= t, 0.0, -1e30).astype(F32)

    def stacked(ref, b, start):
        return jnp.concatenate(
            [ref[b, :, start + g * HD : start + (g + 1) * HD] for g in range(GROUP)], axis=0
        )

    def one(b, base, pack, dq_out, self_out):
        row = (base + b) * NB
        at = [where_ref[row + j] for j in range(NB)]
        q = stacked(pack, b, 0)
        do = stacked(pack, b, GROUP * HD)
        own = 2 * GROUP * HD
        keys = jnp.concatenate([store[i] for i in at] + [pack[b, :, own : own + HD]], axis=0)
        values = jnp.concatenate(
            [store[i + 1] for i in at] + [pack[b, :, own + HD : own + 2 * HD]], axis=0
        )
        bias = jnp.concatenate(
            [
                jnp.full((LP, GROUP * QLEN), jnp.where(valid_ref[row + j] > 0, 0.0, -1e30), F32)
                for j in range(NB)
            ]
            + [causal],
            axis=0,
        )
        scores = dot(keys, q, 1, 1) * SCALE + bias
        top = jnp.max(scores, axis=0, keepdims=True)
        weights = jnp.exp(scores - top)
        probs = weights * (1.0 / jnp.sum(weights, axis=0, keepdims=True))
        low = probs.astype(BF)
        dprob = dot(values, do, 1, 1)
        delta = jnp.sum(probs * dprob, axis=0, keepdims=True)
        dscore = (probs * (dprob - delta)).astype(BF)
        dq = (dot(dscore, keys, 0, 0) * SCALE).astype(BF)
        for g in range(GROUP):
            dq_out[b, :, g * HD : (g + 1) * HD] = dq[g * QLEN : (g + 1) * QLEN]
        dk = (dot(dscore, q, 1, 0) * SCALE).astype(BF)
        dv = dot(low, do, 1, 0).astype(BF)
        self_out[b, :, :HD] = dk[SPAN:]
        self_out[b, :, HD:] = dv[SPAN:]
        for j in range(NB):
            for k, part in enumerate((dk, dv)):
                to = at[j] + k
                grads[to] = (
                    grads[to].astype(F32) + part[j * LP : (j + 1) * LP].astype(F32)
                ).astype(BF)

    def step(b, carry):
        one(b, 0, mine, dq_mine, self_mine)
        one(b, QPD, other, dq_other, self_other)
        return carry

    lax.fori_loop(0, QPD, step, 0)
    stores = [
        pltpu.make_async_copy(grads.at[pl.ds(i * HALF, HALF)], dst, sem_out.at[i])
        for i, dst in enumerate(outs)
    ]
    for copy in stores:
        copy.start()
    for copy in stores:
        copy.wait()


def attention(where, valid, stored, mine, other):
    smem = pl.BlockSpec(memory_space=pltpu.SMEM)
    vmem = pl.BlockSpec(memory_space=pltpu.VMEM)
    hbm = pl.BlockSpec(memory_space=pl.ANY)
    tiles = jax.ShapeDtypeStruct((HALF, LP, HD), BF)
    query = jax.ShapeDtypeStruct((QPD, QLEN, GROUP * HD), BF)
    own = jax.ShapeDtypeStruct((QPD, QLEN, 2 * HD), BF)
    return pl.pallas_call(
        attention_kernel,
        out_shape=(tiles,) * PARTS + (query, query, own, own),
        in_specs=[smem] * 2 + [hbm] * PARTS + [vmem] * 2,
        out_specs=(hbm,) * PARTS + (vmem,) * 4,
        scratch_shapes=[
            pltpu.VMEM((PARTS * HALF, LP, HD), BF),
            pltpu.VMEM((PARTS * HALF, LP, HD), BF),
            pltpu.SemaphoreType.DMA((PARTS,)),
            pltpu.SemaphoreType.DMA((PARTS,)),
        ],
        compiler_params=pltpu.CompilerParams(vmem_limit_bytes=40 * 2**20),
        cost_estimate=pl.CostEstimate(
            flops=16 * 5 * 2 * 272 * 128 * 128, bytes_accessed=12 * 2**20, transcendentals=16 * 272 * 128
        ),
    )(where, valid, *stored, mine, other)


def total(*parts):
    out = parts[0].astype(F32)
    for part in parts[1:]:
        out = out + part.astype(F32)
    return out.astype(BF)


def per_device(
    queries,
    self_key,
    self_value,
    passage_key,
    passage_value,
    out_grad,
    block_ids,
    block_valid,
    passage_slot,
):
    core = lax.axis_index("core")
    my_zl = lax.axis_index("zl")
    swap = ring(2, 1)
    around = ("zh", "zl")
    feat = GROUP * HD

    def head(array, c, width):
        return lax.dynamic_slice_in_dim(array, c * width, width, axis=array.ndim - 1)

    def by_core(mine_part, other_part, axis):
        first = jnp.where(core == 0, mine_part, other_part)
        second = jnp.where(core == 0, other_part, mine_part)
        return jnp.concatenate([first, second], axis=axis)

    code = jnp.concatenate([passage_slot // 16, passage_slot % 16]).astype(BF)
    code_tile = jnp.pad(code.reshape(1, 1, 2), ((0, 0), (0, LP - 1), (0, HD - 2)))

    def passages(c):
        lanes = slice(c * HD, (c + 1) * HD)
        both = jnp.stack([passage_key[:, :, lanes], passage_value[:, :, lanes]], axis=1)
        return jnp.concatenate([both.reshape(TILES, LP, HD), code_tile], axis=0)

    heads = jnp.stack([passages(0), passages(1)])
    far = lax.all_to_all(
        jnp.broadcast_to(heads[None], (ZH, 2, TILES + 1, LP, HD)).reshape(2 * ZH, TILES + 1, LP, HD),
        ("zh", "core"),
        split_axis=0,
        concat_axis=0,
        tiled=True,
    )
    far_halves = far.reshape(2, ZH, TILES + 1, LP, HD)

    def along_x(h):
        return lax.all_to_all(
            jnp.broadcast_to(far_halves[h][None, :, :TILES], (XS, ZH, TILES, LP, HD)),
            "x",
            split_axis=0,
            concat_axis=0,
            tiled=True,
        ).reshape(HALF, LP, HD)

    def up(part):
        return lax.ppermute(part, around, ring(ZS, 1))

    def down(part):
        return lax.ppermute(part, around, ring(ZS, -1))

    s0a, s0b = along_x(0), along_x(1)
    s1a, s3a = down(s0a), up(s0a)
    s3b, s1b = up(s0b), down(s0b)

    def pack(c):
        return jnp.concatenate(
            [
                head(queries, c, feat),
                head(out_grad, c, feat),
                head(self_key, c, HD),
                head(self_value, c, HD),
            ],
            axis=2,
        )

    mine = pack(core)
    other = lax.ppermute(pack(1 - core), "core", swap)
    lists = jnp.stack([block_ids, block_valid])
    lists_other = lax.ppermute(lists, "core", swap)

    codes = far[:, TILES, 0, :2].astype(jnp.int32)
    known = codes[:, 0] * 16 + codes[:, 1]
    known, _ = lax.optimization_barrier((known, s0a[:1, 0, :1]))
    slot_of = lax.all_to_all(
        jnp.broadcast_to(known[None], (XS * ZL * TP, 2 * ZH)),
        ("x", "zl", "tp"),
        split_axis=0,
        concat_axis=0,
        tiled=True,
    ).reshape(-1)
    s1a, slot_of = lax.optimization_barrier((s1a, slot_of))
    s2a, s2b = down(s1a), up(s3b)

    def parts(number):
        pool = number // P_DEV
        z = pool // 2 % ZS
        return pool // (2 * ZS), z // ZL, z % ZL, pool % 2, number % P_DEV

    ids = jnp.concatenate([block_ids, lists_other[0]]).reshape(-1)
    valid = jnp.concatenate([block_valid, lists_other[1]]).reshape(-1)
    x, zh, zl, c, inner = parts(ids)
    id_at = (((x * ZL + zl) * TP + inner) * ZH + zh) * 2 + c
    every = jnp.arange(slot_of.shape[0], dtype=jnp.int32)
    slots = jnp.sum(jnp.where(id_at[:, None] == every[None, :], slot_of[None, :], 0), axis=1)
    x, zh, zl, c, inner = parts(slots)
    part = (zl - my_zl) % ZL * 2 + zh // 2
    where = (((part * XS + x) * 2 + zh % 2) * 2 + c) * TILES + 2 * inner

    *grads, dq_mine, dq_other, self_mine, self_other = attention(
        where, valid, (s0a, s0b, s1a, s1b, s2a, s2b, s3a, s3b), mine, other
    )
    g0a, g0b, g1a, g1b, g2a, g2b, g3a, g3b = grads

    via_a, via_b = up(g2a), down(g2b)
    from_below_b, from_above_a = up(g1b), down(g3a)
    from_below_a = up(total(g1a, via_a))
    from_above_b = down(total(g3b, via_b))
    halves = (XS, ZH, TILES, LP, HD)
    summed = jnp.concatenate(
        [
            total(g0a, from_above_a, from_below_a).reshape(halves),
            total(g0b, from_below_b, from_above_b).reshape(halves),
        ],
        axis=1,
    )
    x_parts = lax.all_to_all(summed, "x", split_axis=0, concat_axis=0, tiled=True)
    x_sum = total(*[x_parts[i] for i in range(XS)])
    far_parts = lax.all_to_all(x_sum, ("zh", "core"), split_axis=0, concat_axis=0, tiled=True)
    far_parts = far_parts.reshape(ZH, 2, P_DEV, 2, LP, HD)
    grad = total(*[far_parts[i] for i in range(ZH)])
    key_grad = jnp.concatenate([grad[0, :, 0], grad[1, :, 0]], axis=2)
    value_grad = jnp.concatenate([grad[0, :, 1], grad[1, :, 1]], axis=2)

    dq_other, self_other, _ = lax.optimization_barrier((dq_other, self_other, from_below_b[:1, 0, :1]))
    dq_taken = lax.ppermute(dq_other, "core", swap)
    self_taken = lax.ppermute(self_other, "core", swap)
    query_grad = by_core(dq_mine, dq_taken, 2)
    self_key_grad = by_core(self_mine[:, :, :HD], self_taken[:, :, :HD], 2)
    self_value_grad = by_core(self_mine[:, :, HD:], self_taken[:, :, HD:], 2)
    return (query_grad, self_key_grad, self_value_grad, key_grad, value_grad)


def solution(mesh):
    fine = Mesh(mesh.devices.reshape(XS, ZH, ZL, 2, TP), ("x", "zh", "zl", "core", "tp"))
    pool = ("x", "zh", "zl", "core")
    rows = P(pool, None, "tp")
    return jax.shard_map(
        per_device,
        mesh=fine,
        in_specs=(rows,) * 6 + (P(pool, None), P(pool, None), P(pool + ("tp",))),
        out_specs=(rows,) * 5,
        check_vma=False,
    )
```

```python
import jax
import jax.numpy as jnp
from jax import lax
from jax.experimental import pallas as pl
from jax.experimental.pallas import tpu as pltpu
from jax.sharding import Mesh
from jax.sharding import PartitionSpec as P

HD = 128
GROUP = 8
QLEN = 16
LP = 16
NB = 16
QPD = 8
P_DEV = 4
XS, ZH, ZL, TP = 4, 4, 4, 4
ZS = ZH * ZL
TILES = 2 * P_DEV
BLOCK = ZH * TILES
HALF = XS * BLOCK
PARTS = 2 * ZL
CODES = TP * ZH * 2
SCALE = HD ** (-0.5)
SPAN = NB * LP
BF = jnp.bfloat16
F32 = jnp.float32


def ring(n, d):
    return [(i, (i + d) % n) for i in range(n)]


def dot(a, b, ca, cb):
    return lax.dot_general(a, b, (((ca,), (cb,)), ((), ())), preferred_element_type=F32)


def attention_kernel(
    where_ref,
    valid_ref,
    *refs,
):
    stored, (mine, other) = refs[:PARTS], refs[PARTS : PARTS + 2]
    outs = refs[PARTS + 2 : 2 * PARTS + 2]
    dq_mine, dq_other, self_mine, self_other = refs[2 * PARTS + 2 : 2 * PARTS + 6]
    store, grads, sem_in, sem_out = refs[2 * PARTS + 6 :]
    loads = []
    for i, src in enumerate(stored):
        pieces = [(0, 0, HALF)] if i % 2 == 0 else [(x * (BLOCK + 1), x * BLOCK, BLOCK) for x in range(XS)]
        for start, to, size in pieces:
            loads.append(
                pltpu.make_async_copy(
                    src.at[pl.ds(start, size)], store.at[pl.ds(i * HALF + to, size)], sem_in.at[len(loads)]
                )
            )
    for copy in loads:
        copy.start()

    def clear(i, carry):
        grads[pl.ds(i * 16, 16)] = jnp.zeros((16, LP, HD), BF)
        return carry

    lax.fori_loop(0, PARTS * HALF // 16, clear, 0)
    for copy in loads:
        copy.wait()

    u = lax.broadcasted_iota(jnp.int32, (QLEN, GROUP * QLEN), 0)
    t = lax.broadcasted_iota(jnp.int32, (QLEN, GROUP * QLEN), 1) % QLEN
    causal = jnp.where(u <= t, 0.0, -1e30).astype(F32)

    def stacked(ref, b, start):
        return jnp.concatenate(
            [ref[b, :, start + g * HD : start + (g + 1) * HD] for g in range(GROUP)], axis=0
        )

    def one(b, base, pack, dq_out, self_out):
        row = (base + b) * NB
        at = [where_ref[row + j] for j in range(NB)]
        q = stacked(pack, b, 0)
        do = stacked(pack, b, GROUP * HD)
        own = 2 * GROUP * HD
        keys = jnp.concatenate([store[i] for i in at] + [pack[b, :, own : own + HD]], axis=0)
        values = jnp.concatenate(
            [store[i + 1] for i in at] + [pack[b, :, own + HD : own + 2 * HD]], axis=0
        )
        bias = jnp.concatenate(
            [
                jnp.full((LP, GROUP * QLEN), jnp.where(valid_ref[row + j] > 0, 0.0, -1e30), F32)
                for j in range(NB)
            ]
            + [causal],
            axis=0,
        )
        scores = dot(keys, q, 1, 1) * SCALE + bias
        top = jnp.max(scores, axis=0, keepdims=True)
        weights = jnp.exp(scores - top)
        probs = weights * (1.0 / jnp.sum(weights, axis=0, keepdims=True))
        low = probs.astype(BF)
        dprob = dot(values, do, 1, 1)
        delta = jnp.sum(probs * dprob, axis=0, keepdims=True)
        dscore = (probs * (dprob - delta)).astype(BF)
        dq = (dot(dscore, keys, 0, 0) * SCALE).astype(BF)
        for g in range(GROUP):
            dq_out[b, :, g * HD : (g + 1) * HD] = dq[g * QLEN : (g + 1) * QLEN]
        dk = (dot(dscore, q, 1, 0) * SCALE).astype(BF)
        dv = dot(low, do, 1, 0).astype(BF)
        self_out[b, :, :HD] = dk[SPAN:]
        self_out[b, :, HD:] = dv[SPAN:]
        for j in range(NB):
            for k, part in enumerate((dk, dv)):
                to = at[j] + k
                grads[to] = (
                    grads[to].astype(F32) + part[j * LP : (j + 1) * LP].astype(F32)
                ).astype(BF)

    def step(b, carry):
        one(b, 0, mine, dq_mine, self_mine)
        one(b, QPD, other, dq_other, self_other)
        return carry

    lax.fori_loop(0, QPD, step, 0)
    stores = [
        pltpu.make_async_copy(grads.at[pl.ds(i * HALF, HALF)], dst, sem_out.at[i])
        for i, dst in enumerate(outs)
    ]
    for copy in stores:
        copy.start()
    for copy in stores:
        copy.wait()


def attention(where, valid, stored, mine, other):
    smem = pl.BlockSpec(memory_space=pltpu.SMEM)
    vmem = pl.BlockSpec(memory_space=pltpu.VMEM)
    hbm = pl.BlockSpec(memory_space=pl.ANY)
    tiles = jax.ShapeDtypeStruct((HALF, LP, HD), BF)
    query = jax.ShapeDtypeStruct((QPD, QLEN, GROUP * HD), BF)
    own = jax.ShapeDtypeStruct((QPD, QLEN, 2 * HD), BF)
    return pl.pallas_call(
        attention_kernel,
        out_shape=(tiles,) * PARTS + (query, query, own, own),
        in_specs=[smem] * 2 + [hbm] * PARTS + [vmem] * 2,
        out_specs=(hbm,) * PARTS + (vmem,) * 4,
        scratch_shapes=[
            pltpu.VMEM((PARTS * HALF, LP, HD), BF),
            pltpu.VMEM((PARTS * HALF, LP, HD), BF),
            pltpu.SemaphoreType.DMA((ZL * (1 + XS),)),
            pltpu.SemaphoreType.DMA((PARTS,)),
        ],
        compiler_params=pltpu.CompilerParams(vmem_limit_bytes=40 * 2**20),
        cost_estimate=pl.CostEstimate(
            flops=16 * 5 * 2 * 272 * 128 * 128, bytes_accessed=12 * 2**20, transcendentals=16 * 272 * 128
        ),
    )(where, valid, *stored, mine, other)


def total(*parts):
    out = parts[0].astype(F32)
    for part in parts[1:]:
        out = out + part.astype(F32)
    return out.astype(BF)


def per_device(
    queries,
    self_key,
    self_value,
    passage_key,
    passage_value,
    out_grad,
    block_ids,
    block_valid,
    passage_slot,
):
    core = lax.axis_index("core")
    my_zl = lax.axis_index("zl")
    my_tp = lax.axis_index("tp")
    swap = ring(2, 1)
    around = ("zh", "zl")
    feat = GROUP * HD

    def head(array, c, width):
        return lax.dynamic_slice_in_dim(array, c * width, width, axis=array.ndim - 1)

    def by_core(mine_part, other_part, axis):
        first = jnp.where(core == 0, mine_part, other_part)
        second = jnp.where(core == 0, other_part, mine_part)
        return jnp.concatenate([first, second], axis=axis)

    code = jnp.concatenate([passage_slot // 16, passage_slot % 16]).astype(BF)
    code_tile = jnp.pad(code.reshape(1, 1, 2), ((0, 0), (0, LP - 1), (0, HD - 2)))

    def passages(c):
        lanes = slice(c * HD, (c + 1) * HD)
        both = jnp.stack([passage_key[:, :, lanes], passage_value[:, :, lanes]], axis=1)
        return jnp.concatenate([both.reshape(TILES, LP, HD), code_tile], axis=0)

    heads = jnp.stack([passages(0), passages(1)])
    far = lax.all_to_all(
        jnp.broadcast_to(heads[None], (ZH, 2, TILES + 1, LP, HD)).reshape(2 * ZH, TILES + 1, LP, HD),
        ("zh", "core"),
        split_axis=0,
        concat_axis=0,
        tiled=True,
    )
    far_halves = far.reshape(2, ZH, TILES + 1, LP, HD)

    def along_x(block):
        return lax.all_to_all(
            jnp.broadcast_to(block[None], (XS,) + block.shape),
            "x",
            split_axis=0,
            concat_axis=0,
            tiled=True,
        ).reshape(-1, LP, HD)

    def up(part):
        return lax.ppermute(part, around, ring(ZS, 1))

    def down(part):
        return lax.ppermute(part, around, ring(ZS, -1))

    s0a = along_x(far_halves[0, :, :TILES].reshape(BLOCK, LP, HD))
    codes = far[:, TILES, 0, :2].astype(jnp.int32)
    known = codes[:, 0] * 16 + codes[:, 1]
    all_known = jnp.concatenate(
        [known] + [lax.ppermute(known, "tp", ring(TP, d)) for d in range(1, TP)]
    )
    coded = jnp.concatenate([all_known // 16, all_known % 16]).astype(BF)
    spread_tile = jnp.pad(coded.reshape(1, 1, 2 * CODES), ((0, 0), (0, LP - 1), (0, HD - 2 * CODES)))
    s0b = along_x(
        jnp.concatenate([far_halves[1, :, :TILES].reshape(BLOCK, LP, HD), spread_tile], axis=0)
    )
    s1a, s3a = down(s0a), up(s0a)
    s3b, s1b = up(s0b), down(s0b)
    s2a, s2b = down(s1a), up(s3b)

    def pack(c):
        return jnp.concatenate(
            [
                head(queries, c, feat),
                head(out_grad, c, feat),
                head(self_key, c, HD),
                head(self_value, c, HD),
            ],
            axis=2,
        )

    mine = pack(core)
    other = lax.ppermute(pack(1 - core), "core", swap)
    lists = jnp.stack([block_ids, block_valid])
    lists_other = lax.ppermute(lists, "core", swap)

    spread = jnp.concatenate(
        [s.reshape(XS, BLOCK + 1, LP, HD)[:, BLOCK, 0, : 2 * CODES] for s in (s0b, s1b, s2b, s3b)]
    ).astype(jnp.int32)
    slot_of = (spread[:, :CODES] * 16 + spread[:, CODES:]).reshape(-1)

    def parts(number):
        pool = number // P_DEV
        z = pool // 2 % ZS
        return pool // (2 * ZS), z // ZL, z % ZL, pool % 2, number % P_DEV

    ids = jnp.concatenate([block_ids, lists_other[0]]).reshape(-1)
    valid = jnp.concatenate([block_valid, lists_other[1]]).reshape(-1)
    x, zh, zl, c, inner = parts(ids)
    id_at = ((((zl - my_zl) % ZL * XS + x) * TP + (my_tp - inner) % TP) * ZH + zh) * 2 + c
    every = jnp.arange(slot_of.shape[0], dtype=jnp.int32)
    slots = jnp.sum(jnp.where(id_at[:, None] == every[None, :], slot_of[None, :], 0), axis=1)
    x, zh, zl, c, inner = parts(slots)
    part = (zl - my_zl) % ZL * 2 + zh // 2
    where = (((part * XS + x) * 2 + zh % 2) * 2 + c) * TILES + 2 * inner

    *grads, dq_mine, dq_other, self_mine, self_other = attention(
        where, valid, (s0a, s0b, s1a, s1b, s2a, s2b, s3a, s3b), mine, other
    )
    g0a, g0b, g1a, g1b, g2a, g2b, g3a, g3b = grads

    via_a, via_b = up(g2a), down(g2b)
    from_below_b, from_above_a = up(g1b), down(g3a)
    from_below_a = up(total(g1a, via_a))
    from_above_b = down(total(g3b, via_b))
    halves = (XS, ZH, TILES, LP, HD)
    summed = jnp.concatenate(
        [
            total(g0a, from_above_a, from_below_a).reshape(halves),
            total(g0b, from_below_b, from_above_b).reshape(halves),
        ],
        axis=1,
    )
    x_parts = lax.all_to_all(summed, "x", split_axis=0, concat_axis=0, tiled=True)
    x_sum = total(*[x_parts[i] for i in range(XS)])
    far_parts = lax.all_to_all(x_sum, ("zh", "core"), split_axis=0, concat_axis=0, tiled=True)
    far_parts = far_parts.reshape(ZH, 2, P_DEV, 2, LP, HD)
    grad = total(*[far_parts[i] for i in range(ZH)])
    key_grad = jnp.concatenate([grad[0, :, 0], grad[1, :, 0]], axis=2)
    value_grad = jnp.concatenate([grad[0, :, 1], grad[1, :, 1]], axis=2)

    dq_taken = lax.ppermute(dq_other, "core", swap)
    self_taken = lax.ppermute(self_other, "core", swap)
    query_grad = by_core(dq_mine, dq_taken, 2)
    self_key_grad = by_core(self_mine[:, :, :HD], self_taken[:, :, :HD], 2)
    self_value_grad = by_core(self_mine[:, :, HD:], self_taken[:, :, HD:], 2)
    return (query_grad, self_key_grad, self_value_grad, key_grad, value_grad)


def solution(mesh):
    fine = Mesh(mesh.devices.reshape(XS, ZH, ZL, 2, TP), ("x", "zh", "zl", "core", "tp"))
    pool = ("x", "zh", "zl", "core")
    rows = P(pool, None, "tp")
    return jax.shard_map(
        per_device,
        mesh=fine,
        in_specs=(rows,) * 6 + (P(pool, None), P(pool, None), P(pool + ("tp",))),
        out_specs=(rows,) * 5,
        check_vma=False,
    )
```

```python
import jax
import jax.numpy as jnp
from jax import lax
from jax.experimental import pallas as pl
from jax.experimental.pallas import tpu as pltpu
from jax.sharding import Mesh
from jax.sharding import PartitionSpec as P

HD = 128
GROUP = 8
QLEN = 16
LP = 16
NB = 16
QPD = 8
P_DEV = 4
XS, ZH, ZL, TP = 4, 4, 4, 4
ZS = ZH * ZL
TILES = 2 * P_DEV
HALF = XS * ZH * TILES
PARTS = 2 * ZL
SCALE = HD ** (-0.5)
SPAN = NB * LP
BF = jnp.bfloat16
F32 = jnp.float32


def ring(n, d):
    return [(i, (i + d) % n) for i in range(n)]


def dot(a, b, ca, cb):
    return lax.dot_general(a, b, (((ca,), (cb,)), ((), ())), preferred_element_type=F32)


def attention_kernel(
    where_ref,
    valid_ref,
    *refs,
):
    stored, (mine, other) = refs[:5], refs[5:7]
    outs = refs[7 : PARTS + 7]
    dq_mine, dq_other, self_mine, self_other = refs[PARTS + 7 : PARTS + 11]
    store, grads, sem_in, sem_out = refs[PARTS + 11 :]
    loads = [
        pltpu.make_async_copy(src, store.at[pl.ds(start * HALF, size * HALF)], sem_in.at[i])
        for i, (src, start, size) in enumerate(zip(stored, (0, 2, 4, 5, 6), (2, 2, 1, 1, 2)))
    ]
    for copy in loads:
        copy.start()

    def clear(i, carry):
        grads[pl.ds(i * 16, 16)] = jnp.zeros((16, LP, HD), BF)
        return carry

    lax.fori_loop(0, PARTS * HALF // 16, clear, 0)
    for copy in loads:
        copy.wait()

    u = lax.broadcasted_iota(jnp.int32, (QLEN, GROUP * QLEN), 0)
    t = lax.broadcasted_iota(jnp.int32, (QLEN, GROUP * QLEN), 1) % QLEN
    causal = jnp.where(u <= t, 0.0, -1e30).astype(F32)

    def stacked(ref, b, start):
        return jnp.concatenate(
            [ref[b, :, start + g * HD : start + (g + 1) * HD] for g in range(GROUP)], axis=0
        )

    def one(b, base, pack, dq_out, self_out):
        row = (base + b) * NB
        at = [where_ref[row + j] for j in range(NB)]
        q = stacked(pack, b, 0)
        do = stacked(pack, b, GROUP * HD)
        own = 2 * GROUP * HD
        keys = jnp.concatenate([store[i] for i in at] + [pack[b, :, own : own + HD]], axis=0)
        values = jnp.concatenate(
            [store[i + 1] for i in at] + [pack[b, :, own + HD : own + 2 * HD]], axis=0
        )
        bias = jnp.concatenate(
            [
                jnp.full((LP, GROUP * QLEN), jnp.where(valid_ref[row + j] > 0, 0.0, -1e30), F32)
                for j in range(NB)
            ]
            + [causal],
            axis=0,
        )
        scores = dot(keys, q, 1, 1) * SCALE + bias
        top = jnp.max(scores, axis=0, keepdims=True)
        weights = jnp.exp(scores - top)
        probs = weights * (1.0 / jnp.sum(weights, axis=0, keepdims=True))
        low = probs.astype(BF)
        dprob = dot(values, do, 1, 1)
        delta = jnp.sum(probs * dprob, axis=0, keepdims=True)
        dscore = (probs * (dprob - delta)).astype(BF)
        dq = (dot(dscore, keys, 0, 0) * SCALE).astype(BF)
        for g in range(GROUP):
            dq_out[b, :, g * HD : (g + 1) * HD] = dq[g * QLEN : (g + 1) * QLEN]
        dk = (dot(dscore, q, 1, 0) * SCALE).astype(BF)
        dv = dot(low, do, 1, 0).astype(BF)
        self_out[b, :, :HD] = dk[SPAN:]
        self_out[b, :, HD:] = dv[SPAN:]
        for j in range(NB):
            for k, part in enumerate((dk, dv)):
                to = at[j] + k
                grads[to] = (
                    grads[to].astype(F32) + part[j * LP : (j + 1) * LP].astype(F32)
                ).astype(BF)

    def step(b, carry):
        one(b, 0, mine, dq_mine, self_mine)
        one(b, QPD, other, dq_other, self_other)
        return carry

    lax.fori_loop(0, QPD, step, 0)
    stores = [
        pltpu.make_async_copy(grads.at[pl.ds(i * HALF, HALF)], dst, sem_out.at[i])
        for i, dst in enumerate(outs)
    ]
    for copy in stores:
        copy.start()
    for copy in stores:
        copy.wait()


def attention(where, valid, stored, mine, other):
    smem = pl.BlockSpec(memory_space=pltpu.SMEM)
    vmem = pl.BlockSpec(memory_space=pltpu.VMEM)
    hbm = pl.BlockSpec(memory_space=pl.ANY)
    tiles = jax.ShapeDtypeStruct((HALF, LP, HD), BF)
    query = jax.ShapeDtypeStruct((QPD, QLEN, GROUP * HD), BF)
    own = jax.ShapeDtypeStruct((QPD, QLEN, 2 * HD), BF)
    return pl.pallas_call(
        attention_kernel,
        out_shape=(tiles,) * PARTS + (query, query, own, own),
        in_specs=[smem] * 2 + [hbm] * 5 + [vmem] * 2,
        out_specs=(hbm,) * PARTS + (vmem,) * 4,
        scratch_shapes=[
            pltpu.VMEM((PARTS * HALF, LP, HD), BF),
            pltpu.VMEM((PARTS * HALF, LP, HD), BF),
            pltpu.SemaphoreType.DMA((5,)),
            pltpu.SemaphoreType.DMA((PARTS,)),
        ],
        compiler_params=pltpu.CompilerParams(vmem_limit_bytes=40 * 2**20),
        cost_estimate=pl.CostEstimate(
            flops=16 * 5 * 2 * 272 * 128 * 128, bytes_accessed=12 * 2**20, transcendentals=16 * 272 * 128
        ),
    )(where, valid, *stored, mine, other)


def total(*parts):
    out = parts[0].astype(F32)
    for part in parts[1:]:
        out = out + part.astype(F32)
    return out.astype(BF)


def per_device(
    queries,
    self_key,
    self_value,
    passage_key,
    passage_value,
    out_grad,
    block_ids,
    block_valid,
    passage_slot,
):
    core = lax.axis_index("core")
    my_zl = lax.axis_index("zl")
    swap = ring(2, 1)
    around = ("zh", "zl")
    feat = GROUP * HD

    def head(array, c, width):
        return lax.dynamic_slice_in_dim(array, c * width, width, axis=array.ndim - 1)

    def by_core(mine_part, other_part, axis):
        first = jnp.where(core == 0, mine_part, other_part)
        second = jnp.where(core == 0, other_part, mine_part)
        return jnp.concatenate([first, second], axis=axis)

    code = jnp.concatenate([passage_slot // 16, passage_slot % 16]).astype(BF)
    code_tile = jnp.pad(code.reshape(1, 1, 2), ((0, 0), (0, LP - 1), (0, HD - 2)))

    def passages(c):
        lanes = slice(c * HD, (c + 1) * HD)
        both = jnp.stack([passage_key[:, :, lanes], passage_value[:, :, lanes]], axis=1)
        return jnp.concatenate([both.reshape(TILES, LP, HD), code_tile], axis=0)

    heads = jnp.stack([passages(0), passages(1)])
    far = lax.all_to_all(
        jnp.broadcast_to(heads[None], (ZH, 2, TILES + 1, LP, HD)).reshape(2 * ZH, TILES + 1, LP, HD),
        ("zh", "core"),
        split_axis=0,
        concat_axis=0,
        tiled=True,
    )
    s0 = lax.all_to_all(
        jnp.broadcast_to(far[None, :, :TILES], (XS, 2 * ZH, TILES, LP, HD)),
        "x",
        split_axis=0,
        concat_axis=0,
        tiled=True,
    ).reshape(2 * HALF, LP, HD)

    def up(part):
        return lax.ppermute(part, around, ring(ZS, 1))

    def down(part):
        return lax.ppermute(part, around, ring(ZS, -1))

    s1, s3 = down(s0), up(s0)

    def pack(c):
        return jnp.concatenate(
            [
                head(queries, c, feat),
                head(out_grad, c, feat),
                head(self_key, c, HD),
                head(self_value, c, HD),
            ],
            axis=2,
        )

    mine = pack(core)
    other = lax.ppermute(pack(1 - core), "core", swap)
    lists = jnp.stack([block_ids, block_valid])
    lists_other = lax.ppermute(lists, "core", swap)

    codes = far[:, TILES, 0, :2].astype(jnp.int32)
    known = codes[:, 0] * 16 + codes[:, 1]
    known = known + jnp.minimum(jnp.abs(s0[0, 0, 0]).astype(jnp.int32), 0)
    slot_of = lax.all_to_all(
        jnp.broadcast_to(known[None], (XS * ZL * TP, 2 * ZH)),
        ("x", "zl", "tp"),
        split_axis=0,
        concat_axis=0,
        tiled=True,
    ).reshape(-1)
    zero = jnp.minimum(slot_of[0], 0)
    s2a = down(lax.dynamic_slice_in_dim(s1, zero, HALF))
    s2b = up(lax.dynamic_slice_in_dim(s3, HALF + zero, HALF))

    def parts(number):
        pool = number // P_DEV
        z = pool // 2 % ZS
        return pool // (2 * ZS), z // ZL, z % ZL, pool % 2, number % P_DEV

    ids = jnp.concatenate([block_ids, lists_other[0]]).reshape(-1)
    valid = jnp.concatenate([block_valid, lists_other[1]]).reshape(-1)
    x, zh, zl, c, inner = parts(ids)
    id_at = (((x * ZL + zl) * TP + inner) * ZH + zh) * 2 + c
    every = jnp.arange(slot_of.shape[0], dtype=jnp.int32)
    slots = jnp.sum(jnp.where(id_at[:, None] == every[None, :], slot_of[None, :], 0), axis=1)
    x, zh, zl, c, inner = parts(slots)
    where = ((((zl - my_zl) % ZL * XS + x) * ZH + zh) * 2 + c) * TILES + 2 * inner

    *grads, dq_mine, dq_other, self_mine, self_other = attention(
        where, valid, (s0, s1, s2a, s2b, s3), mine, other
    )
    g0a, g0b, g1a, g1b, g2a, g2b, g3a, g3b = grads

    via_a, via_b = up(g2a), down(g2b)
    from_below_b, from_above_a = up(g1b), down(g3a)
    from_below_a = up(total(g1a, via_a))
    from_above_b = down(total(g3b, via_b))
    summed = jnp.concatenate(
        [total(g0a, from_above_a, from_below_a), total(g0b, from_below_b, from_above_b)]
    ).reshape(XS, 2 * ZH, TILES, LP, HD)
    x_parts = lax.all_to_all(summed, "x", split_axis=0, concat_axis=0, tiled=True)
    x_sum = total(*[x_parts[i] for i in range(XS)])
    far_parts = lax.all_to_all(x_sum, ("zh", "core"), split_axis=0, concat_axis=0, tiled=True)
    far_parts = far_parts.reshape(ZH, 2, P_DEV, 2, LP, HD)
    grad = total(*[far_parts[i] for i in range(ZH)])
    key_grad = jnp.concatenate([grad[0, :, 0], grad[1, :, 0]], axis=2)
    value_grad = jnp.concatenate([grad[0, :, 1], grad[1, :, 1]], axis=2)

    dq_taken = lax.ppermute(dq_other, "core", swap)
    self_taken = lax.ppermute(self_other, "core", swap)
    query_grad = by_core(dq_mine, dq_taken, 2)
    self_key_grad = by_core(self_mine[:, :, :HD], self_taken[:, :, :HD], 2)
    self_value_grad = by_core(self_mine[:, :, HD:], self_taken[:, :, HD:], 2)
    return (query_grad, self_key_grad, self_value_grad, key_grad, value_grad)


def solution(mesh):
    fine = Mesh(mesh.devices.reshape(XS, ZH, ZL, 2, TP), ("x", "zh", "zl", "core", "tp"))
    pool = ("x", "zh", "zl", "core")
    rows = P(pool, None, "tp")
    return jax.shard_map(
        per_device,
        mesh=fine,
        in_specs=(rows,) * 6 + (P(pool, None), P(pool, None), P(pool + ("tp",))),
        out_specs=(rows,) * 5,
        check_vma=False,
    )
```

```python
import jax
import jax.numpy as jnp
from jax import lax
from jax.experimental import pallas as pl
from jax.experimental.pallas import tpu as pltpu
from jax.sharding import Mesh
from jax.sharding import PartitionSpec as P

HD = 128
GROUP = 8
QLEN = 16
LP = 16
NB = 16
QPD = 8
P_DEV = 4
XS, ZH, ZL, TP = 4, 4, 4, 4
ZS = ZH * ZL
TILES = 2 * P_DEV
BLOCK = 2 * ZH * TILES
HALF = XS // 2 * BLOCK
PARTS = 2 * ZL
CODES = 4 * ZH
SCALE = HD ** (-0.5)
SPAN = NB * LP
BF = jnp.bfloat16
F32 = jnp.float32


def ring(n, d):
    return [(i, (i + d) % n) for i in range(n)]


def dot(a, b, ca, cb):
    return lax.dot_general(a, b, (((ca,), (cb,)), ((), ())), preferred_element_type=F32)


def attention_kernel(
    where_ref,
    valid_ref,
    *refs,
):
    stored, (mine, other) = refs[:5], refs[5:7]
    outs = refs[7 : PARTS + 7]
    dq_mine, dq_other, self_mine, self_other = refs[PARTS + 7 : PARTS + 11]
    store, grads, sem_in, sem_out = refs[PARTS + 11 :]
    loads, to = [], 0
    for src in stored:
        for i in range(src.shape[0] // (BLOCK + 1)):
            loads.append(
                pltpu.make_async_copy(
                    src.at[pl.ds(i * (BLOCK + 1), BLOCK)], store.at[pl.ds(to, BLOCK)], sem_in.at[to // BLOCK]
                )
            )
            to += BLOCK
    for copy in loads:
        copy.start()

    def clear(i, carry):
        grads[pl.ds(i * 16, 16)] = jnp.zeros((16, LP, HD), BF)
        return carry

    lax.fori_loop(0, PARTS * HALF // 16, clear, 0)
    for copy in loads:
        copy.wait()

    u = lax.broadcasted_iota(jnp.int32, (QLEN, GROUP * QLEN), 0)
    t = lax.broadcasted_iota(jnp.int32, (QLEN, GROUP * QLEN), 1) % QLEN
    causal = jnp.where(u <= t, 0.0, -1e30).astype(F32)

    def stacked(ref, b, start):
        return jnp.concatenate(
            [ref[b, :, start + g * HD : start + (g + 1) * HD] for g in range(GROUP)], axis=0
        )

    def one(b, base, pack, dq_out, self_out):
        row = (base + b) * NB
        at = [where_ref[row + j] for j in range(NB)]
        q = stacked(pack, b, 0)
        do = stacked(pack, b, GROUP * HD)
        own = 2 * GROUP * HD
        keys = jnp.concatenate([store[i] for i in at] + [pack[b, :, own : own + HD]], axis=0)
        values = jnp.concatenate(
            [store[i + 1] for i in at] + [pack[b, :, own + HD : own + 2 * HD]], axis=0
        )
        bias = jnp.concatenate(
            [
                jnp.full((LP, GROUP * QLEN), jnp.where(valid_ref[row + j] > 0, 0.0, -1e30), F32)
                for j in range(NB)
            ]
            + [causal],
            axis=0,
        )
        scores = dot(keys, q, 1, 1) * SCALE + bias
        top = jnp.max(scores, axis=0, keepdims=True)
        weights = jnp.exp(scores - top)
        probs = weights * (1.0 / jnp.sum(weights, axis=0, keepdims=True))
        low = probs.astype(BF)
        dprob = dot(values, do, 1, 1)
        delta = jnp.sum(probs * dprob, axis=0, keepdims=True)
        dscore = (probs * (dprob - delta)).astype(BF)
        dq = (dot(dscore, keys, 0, 0) * SCALE).astype(BF)
        for g in range(GROUP):
            dq_out[b, :, g * HD : (g + 1) * HD] = dq[g * QLEN : (g + 1) * QLEN]
        dk = (dot(dscore, q, 1, 0) * SCALE).astype(BF)
        dv = dot(low, do, 1, 0).astype(BF)
        self_out[b, :, :HD] = dk[SPAN:]
        self_out[b, :, HD:] = dv[SPAN:]
        for j in range(NB):
            for k, part in enumerate((dk, dv)):
                to = at[j] + k
                grads[to] = (
                    grads[to].astype(F32) + part[j * LP : (j + 1) * LP].astype(F32)
                ).astype(BF)

    def step(b, carry):
        one(b, 0, mine, dq_mine, self_mine)
        one(b, QPD, other, dq_other, self_other)
        return carry

    lax.fori_loop(0, QPD, step, 0)
    stores = [
        pltpu.make_async_copy(grads.at[pl.ds(i * HALF, HALF)], dst, sem_out.at[i])
        for i, dst in enumerate(outs)
    ]
    for copy in stores:
        copy.start()
    for copy in stores:
        copy.wait()


def attention(where, valid, stored, mine, other):
    smem = pl.BlockSpec(memory_space=pltpu.SMEM)
    vmem = pl.BlockSpec(memory_space=pltpu.VMEM)
    hbm = pl.BlockSpec(memory_space=pl.ANY)
    tiles = jax.ShapeDtypeStruct((HALF, LP, HD), BF)
    query = jax.ShapeDtypeStruct((QPD, QLEN, GROUP * HD), BF)
    own = jax.ShapeDtypeStruct((QPD, QLEN, 2 * HD), BF)
    return pl.pallas_call(
        attention_kernel,
        out_shape=(tiles,) * PARTS + (query, query, own, own),
        in_specs=[smem] * 2 + [hbm] * 5 + [vmem] * 2,
        out_specs=(hbm,) * PARTS + (vmem,) * 4,
        scratch_shapes=[
            pltpu.VMEM((PARTS * HALF, LP, HD), BF),
            pltpu.VMEM((PARTS * HALF, LP, HD), BF),
            pltpu.SemaphoreType.DMA((ZL * XS,)),
            pltpu.SemaphoreType.DMA((PARTS,)),
        ],
        compiler_params=pltpu.CompilerParams(vmem_limit_bytes=40 * 2**20),
        cost_estimate=pl.CostEstimate(
            flops=16 * 5 * 2 * 272 * 128 * 128, bytes_accessed=12 * 2**20, transcendentals=16 * 272 * 128
        ),
    )(where, valid, *stored, mine, other)


def total(*parts):
    out = parts[0].astype(F32)
    for part in parts[1:]:
        out = out + part.astype(F32)
    return out.astype(BF)


def per_device(
    queries,
    self_key,
    self_value,
    passage_key,
    passage_value,
    out_grad,
    block_ids,
    block_valid,
    passage_slot,
):
    core = lax.axis_index("core")
    my_zl = lax.axis_index("zl")
    swap = ring(2, 1)
    around = ("zh", "zl")
    feat = GROUP * HD

    def head(array, c, width):
        return lax.dynamic_slice_in_dim(array, c * width, width, axis=array.ndim - 1)

    def by_core(mine_part, other_part, axis):
        first = jnp.where(core == 0, mine_part, other_part)
        second = jnp.where(core == 0, other_part, mine_part)
        return jnp.concatenate([first, second], axis=axis)

    lane = lax.broadcasted_iota(jnp.int32, (1, LP, HD), 2)
    at = 4 * lax.axis_index("zh") + 2 * core
    code_tile = jnp.where(lane == at, passage_slot // 16, jnp.where(lane == at + 1, passage_slot % 16, 0))
    code_tile = code_tile.astype(BF)

    def passages(c):
        lanes = slice(c * HD, (c + 1) * HD)
        both = jnp.stack([passage_key[:, :, lanes], passage_value[:, :, lanes]], axis=1)
        return jnp.concatenate([both.reshape(TILES, LP, HD), code_tile], axis=0)

    heads = jnp.stack([passages(0), passages(1)])
    far = lax.all_to_all(
        jnp.broadcast_to(heads[None], (ZH, 2, TILES + 1, LP, HD)).reshape(2 * ZH, TILES + 1, LP, HD),
        ("zh", "core"),
        split_axis=0,
        concat_axis=0,
        tiled=True,
    )
    codes = jnp.sum(far[:, TILES:].astype(F32), axis=0).astype(BF)
    block = jnp.concatenate([far[:, :TILES].reshape(BLOCK, LP, HD), codes], axis=0)
    s0 = lax.all_to_all(
        jnp.broadcast_to(block[None], (XS, BLOCK + 1, LP, HD)),
        "x",
        split_axis=0,
        concat_axis=0,
        tiled=True,
    ).reshape(XS * (BLOCK + 1), LP, HD)

    def up(part):
        return lax.ppermute(part, around, ring(ZS, 1))

    def down(part):
        return lax.ppermute(part, around, ring(ZS, -1))

    s1, s3 = down(s0), up(s0)
    half = s0.shape[0] // 2
    s2a, s2b = down(s1[:half]), up(s3[half:])

    def pack(c):
        return jnp.concatenate(
            [
                head(queries, c, feat),
                head(out_grad, c, feat),
                head(self_key, c, HD),
                head(self_value, c, HD),
            ],
            axis=2,
        )

    mine = pack(core)
    other = lax.ppermute(pack(1 - core), "core", swap)
    lists = jnp.stack([block_ids, block_valid])
    lists_other = lax.ppermute(lists, "core", swap)

    def codes_of(part):
        return part.reshape(XS, BLOCK + 1, LP, HD)[:, BLOCK, 0, :CODES]

    c0 = codes_of(s0)
    c2 = lax.ppermute(c0, around, ring(ZS, 2))
    seen = jnp.stack([c0, codes_of(s1), c2, codes_of(s3)]).astype(jnp.int32).reshape(-1, 2)
    known = seen[:, 0] * 16 + seen[:, 1]
    slot_of = lax.all_to_all(
        jnp.broadcast_to(known[None], (TP,) + known.shape), "tp", split_axis=0, concat_axis=0, tiled=True
    ).reshape(-1)

    def parts(number):
        pool = number // P_DEV
        z = pool // 2 % ZS
        return pool // (2 * ZS), z // ZL, z % ZL, pool % 2, number % P_DEV

    ids = jnp.concatenate([block_ids, lists_other[0]]).reshape(-1)
    valid = jnp.concatenate([block_valid, lists_other[1]]).reshape(-1)
    x, zh, zl, c, inner = parts(ids)
    id_at = (((inner * ZL + (zl - my_zl) % ZL) * XS + x) * ZH + zh) * 2 + c
    every = jnp.arange(slot_of.shape[0], dtype=jnp.int32)
    slots = jnp.sum(jnp.where(id_at[:, None] == every[None, :], slot_of[None, :], 0), axis=1)
    x, zh, zl, c, inner = parts(slots)
    where = ((((zl - my_zl) % ZL * XS + x) * ZH + zh) * 2 + c) * TILES + 2 * inner

    *grads, dq_mine, dq_other, self_mine, self_other = attention(
        where, valid, (s0, s1, s2a, s2b, s3), mine, other
    )
    g0a, g0b, g1a, g1b, g2a, g2b, g3a, g3b = grads

    via_a, via_b = up(g2a), down(g2b)
    from_below_b, from_above_a = up(g1b), down(g3a)
    from_below_a = up(total(g1a, via_a))
    from_above_b = down(total(g3b, via_b))
    summed = jnp.concatenate(
        [total(g0a, from_above_a, from_below_a), total(g0b, from_below_b, from_above_b)]
    ).reshape(XS, 2 * ZH, TILES, LP, HD)
    x_parts = lax.all_to_all(summed, "x", split_axis=0, concat_axis=0, tiled=True)
    x_sum = total(*[x_parts[i] for i in range(XS)])
    far_parts = lax.all_to_all(x_sum, ("zh", "core"), split_axis=0, concat_axis=0, tiled=True)
    far_parts = far_parts.reshape(ZH, 2, P_DEV, 2, LP, HD)
    grad = total(*[far_parts[i] for i in range(ZH)])
    key_grad = jnp.concatenate([grad[0, :, 0], grad[1, :, 0]], axis=2)
    value_grad = jnp.concatenate([grad[0, :, 1], grad[1, :, 1]], axis=2)

    dq_taken = lax.ppermute(dq_other, "core", swap)
    self_taken = lax.ppermute(self_other, "core", swap)
    query_grad = by_core(dq_mine, dq_taken, 2)
    self_key_grad = by_core(self_mine[:, :, :HD], self_taken[:, :, :HD], 2)
    self_value_grad = by_core(self_mine[:, :, HD:], self_taken[:, :, HD:], 2)
    return (query_grad, self_key_grad, self_value_grad, key_grad, value_grad)


def solution(mesh):
    fine = Mesh(mesh.devices.reshape(XS, ZH, ZL, 2, TP), ("x", "zh", "zl", "core", "tp"))
    pool = ("x", "zh", "zl", "core")
    rows = P(pool, None, "tp")
    return jax.shard_map(
        per_device,
        mesh=fine,
        in_specs=(rows,) * 6 + (P(pool, None), P(pool, None), P(pool + ("tp",))),
        out_specs=(rows,) * 5,
        check_vma=False,
    )
```

```python
import jax
import jax.numpy as jnp
from jax import lax
from jax.experimental import pallas as pl
from jax.experimental.pallas import tpu as pltpu
from jax.sharding import Mesh
from jax.sharding import PartitionSpec as P

HD = 128
GROUP = 8
QLEN = 16
LP = 16
NB = 16
QPD = 8
P_DEV = 4
XS, ZH, ZL, TP = 4, 4, 4, 4
ZS = ZH * ZL
TILES = 2 * P_DEV
BLOCK = 2 * ZH * TILES
HALF = XS // 2 * BLOCK
PARTS = 2 * ZL
CODES = 4 * ZH
LOADS = 2 * ZL - 1
SCALE = HD ** (-0.5)
SPAN = NB * LP
BF = jnp.bfloat16
F32 = jnp.float32


def ring(n, d):
    return [(i, (i + d) % n) for i in range(n)]


def dot(a, b, ca, cb):
    return lax.dot_general(a, b, (((ca,), (cb,)), ((), ())), preferred_element_type=F32)


def attention_kernel(
    where_ref,
    valid_ref,
    *refs,
):
    stored, (mine, other) = refs[:LOADS], refs[LOADS : LOADS + 2]
    outs = refs[LOADS + 2 : LOADS + 2 + PARTS]
    dq_mine, dq_other, self_mine, self_other = refs[LOADS + 2 + PARTS : LOADS + 6 + PARTS]
    store, grads, sem_in, sem_out = refs[LOADS + 6 + PARTS :]
    loads, to = [], 0
    for src in stored:
        for i in range(src.shape[0] // (BLOCK + 1)):
            loads.append(
                pltpu.make_async_copy(
                    src.at[pl.ds(i * (BLOCK + 1), BLOCK)], store.at[pl.ds(to, BLOCK)], sem_in.at[to // BLOCK]
                )
            )
            to += BLOCK
    for copy in loads:
        copy.start()

    def clear(i, carry):
        grads[pl.ds(i * 16, 16)] = jnp.zeros((16, LP, HD), BF)
        return carry

    lax.fori_loop(0, PARTS * HALF // 16, clear, 0)
    for copy in loads:
        copy.wait()

    u = lax.broadcasted_iota(jnp.int32, (QLEN, GROUP * QLEN), 0)
    t = lax.broadcasted_iota(jnp.int32, (QLEN, GROUP * QLEN), 1) % QLEN
    causal = jnp.where(u <= t, 0.0, -1e30).astype(F32)

    def stacked(ref, b, start):
        return jnp.concatenate(
            [ref[b, :, start + g * HD : start + (g + 1) * HD] for g in range(GROUP)], axis=0
        )

    def one(b, base, pack, dq_out, self_out):
        row = (base + b) * NB
        at = [where_ref[row + j] for j in range(NB)]
        q = stacked(pack, b, 0)
        do = stacked(pack, b, GROUP * HD)
        own = 2 * GROUP * HD
        keys = jnp.concatenate([store[i] for i in at] + [pack[b, :, own : own + HD]], axis=0)
        values = jnp.concatenate(
            [store[i + 1] for i in at] + [pack[b, :, own + HD : own + 2 * HD]], axis=0
        )
        bias = jnp.concatenate(
            [
                jnp.full((LP, GROUP * QLEN), jnp.where(valid_ref[row + j] > 0, 0.0, -1e30), F32)
                for j in range(NB)
            ]
            + [causal],
            axis=0,
        )
        scores = dot(keys, q, 1, 1) * SCALE + bias
        top = jnp.max(scores, axis=0, keepdims=True)
        weights = jnp.exp(scores - top)
        probs = weights * (1.0 / jnp.sum(weights, axis=0, keepdims=True))
        low = probs.astype(BF)
        dprob = dot(values, do, 1, 1)
        delta = jnp.sum(probs * dprob, axis=0, keepdims=True)
        dscore = (probs * (dprob - delta)).astype(BF)
        dq = (dot(dscore, keys, 0, 0) * SCALE).astype(BF)
        for g in range(GROUP):
            dq_out[b, :, g * HD : (g + 1) * HD] = dq[g * QLEN : (g + 1) * QLEN]
        dk = (dot(dscore, q, 1, 0) * SCALE).astype(BF)
        dv = dot(low, do, 1, 0).astype(BF)
        self_out[b, :, :HD] = dk[SPAN:]
        self_out[b, :, HD:] = dv[SPAN:]
        for j in range(NB):
            for k, part in enumerate((dk, dv)):
                to = at[j] + k
                grads[to] = (
                    grads[to].astype(F32) + part[j * LP : (j + 1) * LP].astype(F32)
                ).astype(BF)

    def step(b, carry):
        one(b, 0, mine, dq_mine, self_mine)
        one(b, QPD, other, dq_other, self_other)
        return carry

    lax.fori_loop(0, QPD, step, 0)
    stores = [
        pltpu.make_async_copy(grads.at[pl.ds(i * HALF, HALF)], dst, sem_out.at[i])
        for i, dst in enumerate(outs)
    ]
    for copy in stores:
        copy.start()
    for copy in stores:
        copy.wait()


def attention(where, valid, stored, mine, other):
    smem = pl.BlockSpec(memory_space=pltpu.SMEM)
    vmem = pl.BlockSpec(memory_space=pltpu.VMEM)
    hbm = pl.BlockSpec(memory_space=pl.ANY)
    tiles = jax.ShapeDtypeStruct((HALF, LP, HD), BF)
    query = jax.ShapeDtypeStruct((QPD, QLEN, GROUP * HD), BF)
    own = jax.ShapeDtypeStruct((QPD, QLEN, 2 * HD), BF)
    return pl.pallas_call(
        attention_kernel,
        out_shape=(tiles,) * PARTS + (query, query, own, own),
        in_specs=[smem] * 2 + [hbm] * LOADS + [vmem] * 2,
        out_specs=(hbm,) * PARTS + (vmem,) * 4,
        scratch_shapes=[
            pltpu.VMEM((PARTS * HALF, LP, HD), BF),
            pltpu.VMEM((PARTS * HALF, LP, HD), BF),
            pltpu.SemaphoreType.DMA((ZL * XS,)),
            pltpu.SemaphoreType.DMA((PARTS,)),
        ],
        compiler_params=pltpu.CompilerParams(vmem_limit_bytes=40 * 2**20),
        cost_estimate=pl.CostEstimate(
            flops=16 * 5 * 2 * 272 * 128 * 128, bytes_accessed=12 * 2**20, transcendentals=16 * 272 * 128
        ),
    )(where, valid, *stored, mine, other)


def total(*parts):
    out = parts[0].astype(F32)
    for part in parts[1:]:
        out = out + part.astype(F32)
    return out.astype(BF)


def per_device(
    queries,
    self_key,
    self_value,
    passage_key,
    passage_value,
    out_grad,
    block_ids,
    block_valid,
    passage_slot,
):
    core = lax.axis_index("core")
    my_zl = lax.axis_index("zl")
    swap = ring(2, 1)
    around = ("zh", "zl")
    feat = GROUP * HD

    def head(array, c, width):
        return lax.dynamic_slice_in_dim(array, c * width, width, axis=array.ndim - 1)

    def by_core(mine_part, other_part, axis):
        first = jnp.where(core == 0, mine_part, other_part)
        second = jnp.where(core == 0, other_part, mine_part)
        return jnp.concatenate([first, second], axis=axis)

    lane = lax.broadcasted_iota(jnp.int32, (1, LP, HD), 2)
    at = 4 * lax.axis_index("zh") + 2 * core
    code_tile = jnp.where(lane == at, passage_slot // 16, jnp.where(lane == at + 1, passage_slot % 16, 0))
    code_tile = code_tile.astype(BF)

    def passages(c):
        lanes = slice(c * HD, (c + 1) * HD)
        both = jnp.stack([passage_key[:, :, lanes], passage_value[:, :, lanes]], axis=1)
        return jnp.concatenate([both.reshape(TILES, LP, HD), code_tile], axis=0)

    heads = jnp.stack([passages(0), passages(1)])
    far = lax.all_to_all(
        jnp.broadcast_to(heads[None], (ZH, 2, TILES + 1, LP, HD)).reshape(2 * ZH, TILES + 1, LP, HD),
        ("zh", "core"),
        split_axis=0,
        concat_axis=0,
        tiled=True,
    )
    codes = jnp.sum(far[:, TILES:].astype(F32), axis=0).astype(BF)
    block = jnp.concatenate([far[:, :TILES].reshape(BLOCK, LP, HD), codes], axis=0)
    s0 = lax.all_to_all(
        jnp.broadcast_to(block[None], (XS, BLOCK + 1, LP, HD)),
        "x",
        split_axis=0,
        concat_axis=0,
        tiled=True,
    ).reshape(XS * (BLOCK + 1), LP, HD)

    def up(part):
        return lax.ppermute(part, around, ring(ZS, 1))

    def down(part):
        return lax.ppermute(part, around, ring(ZS, -1))

    half = s0.shape[0] // 2
    s1a, s3b = down(s0[:half]), up(s0[half:])
    s2a, s2b = down(s1a), up(s3b)
    s1b, s3a = down(s0[half:]), up(s0[:half])

    def pack(c):
        return jnp.concatenate(
            [
                head(queries, c, feat),
                head(out_grad, c, feat),
                head(self_key, c, HD),
                head(self_value, c, HD),
            ],
            axis=2,
        )

    mine = pack(core)
    other = lax.ppermute(pack(1 - core), "core", swap)
    lists = jnp.stack([block_ids, block_valid])
    lists_other = lax.ppermute(lists, "core", swap)

    def codes_of(part):
        return part.reshape(-1, BLOCK + 1, LP, HD)[:, BLOCK, 0, :CODES]

    c0 = codes_of(s0)
    c2 = lax.ppermute(c0, around, ring(ZS, 2))
    seen = jnp.concatenate([c0, codes_of(s1a), codes_of(s1b), c2, codes_of(s3a), codes_of(s3b)])
    seen = seen.astype(jnp.int32).reshape(-1, 2)
    known = seen[:, 0] * 16 + seen[:, 1]
    slot_of = lax.all_to_all(
        jnp.broadcast_to(known[None], (TP,) + known.shape), "tp", split_axis=0, concat_axis=0, tiled=True
    ).reshape(-1)

    def parts(number):
        pool = number // P_DEV
        z = pool // 2 % ZS
        return pool // (2 * ZS), z // ZL, z % ZL, pool % 2, number % P_DEV

    ids = jnp.concatenate([block_ids, lists_other[0]]).reshape(-1)
    valid = jnp.concatenate([block_valid, lists_other[1]]).reshape(-1)
    x, zh, zl, c, inner = parts(ids)
    id_at = (((inner * ZL + (zl - my_zl) % ZL) * XS + x) * ZH + zh) * 2 + c
    every = jnp.arange(slot_of.shape[0], dtype=jnp.int32)
    slots = jnp.sum(jnp.where(id_at[:, None] == every[None, :], slot_of[None, :], 0), axis=1)
    x, zh, zl, c, inner = parts(slots)
    where = ((((zl - my_zl) % ZL * XS + x) * ZH + zh) * 2 + c) * TILES + 2 * inner

    *grads, dq_mine, dq_other, self_mine, self_other = attention(
        where, valid, (s0, s1a, s1b, s2a, s2b, s3a, s3b), mine, other
    )
    g0a, g0b, g1a, g1b, g2a, g2b, g3a, g3b = grads

    via_a, via_b = up(g2a), down(g2b)
    from_below_b, from_above_a = up(g1b), down(g3a)
    from_below_a = up(total(g1a, via_a))
    from_above_b = down(total(g3b, via_b))
    summed = jnp.concatenate(
        [total(g0a, from_above_a, from_below_a), total(g0b, from_below_b, from_above_b)]
    ).reshape(XS, 2 * ZH, TILES, LP, HD)
    x_parts = lax.all_to_all(summed, "x", split_axis=0, concat_axis=0, tiled=True)
    x_sum = total(*[x_parts[i] for i in range(XS)])
    far_parts = lax.all_to_all(x_sum, ("zh", "core"), split_axis=0, concat_axis=0, tiled=True)
    far_parts = far_parts.reshape(ZH, 2, P_DEV, 2, LP, HD)
    grad = total(*[far_parts[i] for i in range(ZH)])
    key_grad = jnp.concatenate([grad[0, :, 0], grad[1, :, 0]], axis=2)
    value_grad = jnp.concatenate([grad[0, :, 1], grad[1, :, 1]], axis=2)

    dq_taken = lax.ppermute(dq_other, "core", swap)
    self_taken = lax.ppermute(self_other, "core", swap)
    query_grad = by_core(dq_mine, dq_taken, 2)
    self_key_grad = by_core(self_mine[:, :, :HD], self_taken[:, :, :HD], 2)
    self_value_grad = by_core(self_mine[:, :, HD:], self_taken[:, :, HD:], 2)
    return (query_grad, self_key_grad, self_value_grad, key_grad, value_grad)


def solution(mesh):
    fine = Mesh(mesh.devices.reshape(XS, ZH, ZL, 2, TP), ("x", "zh", "zl", "core", "tp"))
    pool = ("x", "zh", "zl", "core")
    rows = P(pool, None, "tp")
    return jax.shard_map(
        per_device,
        mesh=fine,
        in_specs=(rows,) * 6 + (P(pool, None), P(pool, None), P(pool + ("tp",))),
        out_specs=(rows,) * 5,
        check_vma=False,
    )
```

```python
import jax
import jax.numpy as jnp
from jax import lax
from jax.experimental import pallas as pl
from jax.experimental.pallas import tpu as pltpu
from jax.sharding import Mesh
from jax.sharding import PartitionSpec as P

HD = 128
GROUP = 8
QLEN = 16
LP = 16
NB = 16
QPD = 8
P_DEV = 4
XS, ZH, ZL, TP = 4, 4, 4, 4
ZS = ZH * ZL
TILES = 2 * P_DEV
BLOCK = 2 * ZH * TILES
HALF = XS // 2 * BLOCK
PARTS = 2 * ZL
CODES = 4 * ZH
LOADS = 2 * ZL - 1
SCALE = HD ** (-0.5)
SPAN = NB * LP
BF = jnp.bfloat16
F32 = jnp.float32


def ring(n, d):
    return [(i, (i + d) % n) for i in range(n)]


def dot(a, b, ca, cb):
    return lax.dot_general(a, b, (((ca,), (cb,)), ((), ())), preferred_element_type=F32)


def attention_kernel(
    where_ref,
    valid_ref,
    *refs,
):
    stored, (mine, other) = refs[:LOADS], refs[LOADS : LOADS + 2]
    outs = refs[LOADS + 2 : LOADS + 2 + PARTS]
    dq_mine, dq_other, self_mine, self_other = refs[LOADS + 2 + PARTS : LOADS + 6 + PARTS]
    store, grads, sem_in, sem_out = refs[LOADS + 6 + PARTS :]
    half = BLOCK // 2
    loads = []
    for i, src in enumerate(stored):
        size = BLOCK if i == 0 else half
        first = 0 if i == 0 else (i + 1) // 2 * XS * BLOCK + (i + 1) % 2 * half
        for x in range(XS):
            loads.append(
                pltpu.make_async_copy(
                    src.at[pl.ds(x * (size + 1), size)],
                    store.at[pl.ds(first + x * BLOCK, size)],
                    sem_in.at[i * XS + x],
                )
            )
    for copy in loads:
        copy.start()

    def clear(i, carry):
        grads[pl.ds(i * 16, 16)] = jnp.zeros((16, LP, HD), BF)
        return carry

    lax.fori_loop(0, PARTS * HALF // 16, clear, 0)
    for copy in loads:
        copy.wait()

    u = lax.broadcasted_iota(jnp.int32, (QLEN, GROUP * QLEN), 0)
    t = lax.broadcasted_iota(jnp.int32, (QLEN, GROUP * QLEN), 1) % QLEN
    causal = jnp.where(u <= t, 0.0, -1e30).astype(F32)

    def stacked(ref, b, start):
        return jnp.concatenate(
            [ref[b, :, start + g * HD : start + (g + 1) * HD] for g in range(GROUP)], axis=0
        )

    def one(b, base, pack, dq_out, self_out):
        row = (base + b) * NB
        at = [where_ref[row + j] for j in range(NB)]
        q = stacked(pack, b, 0)
        do = stacked(pack, b, GROUP * HD)
        own = 2 * GROUP * HD
        keys = jnp.concatenate([store[i] for i in at] + [pack[b, :, own : own + HD]], axis=0)
        values = jnp.concatenate(
            [store[i + 1] for i in at] + [pack[b, :, own + HD : own + 2 * HD]], axis=0
        )
        bias = jnp.concatenate(
            [
                jnp.full((LP, GROUP * QLEN), jnp.where(valid_ref[row + j] > 0, 0.0, -1e30), F32)
                for j in range(NB)
            ]
            + [causal],
            axis=0,
        )
        scores = dot(keys, q, 1, 1) * SCALE + bias
        top = jnp.max(scores, axis=0, keepdims=True)
        weights = jnp.exp(scores - top)
        probs = weights * (1.0 / jnp.sum(weights, axis=0, keepdims=True))
        low = probs.astype(BF)
        dprob = dot(values, do, 1, 1)
        delta = jnp.sum(probs * dprob, axis=0, keepdims=True)
        dscore = (probs * (dprob - delta)).astype(BF)
        dq = (dot(dscore, keys, 0, 0) * SCALE).astype(BF)
        for g in range(GROUP):
            dq_out[b, :, g * HD : (g + 1) * HD] = dq[g * QLEN : (g + 1) * QLEN]
        dk = (dot(dscore, q, 1, 0) * SCALE).astype(BF)
        dv = dot(low, do, 1, 0).astype(BF)
        self_out[b, :, :HD] = dk[SPAN:]
        self_out[b, :, HD:] = dv[SPAN:]
        for j in range(NB):
            for k, part in enumerate((dk, dv)):
                to = at[j] + k
                grads[to] = (
                    grads[to].astype(F32) + part[j * LP : (j + 1) * LP].astype(F32)
                ).astype(BF)

    def step(b, carry):
        one(b, 0, mine, dq_mine, self_mine)
        one(b, QPD, other, dq_other, self_other)
        return carry

    lax.fori_loop(0, QPD, step, 0)
    stores = [
        pltpu.make_async_copy(grads.at[pl.ds(i * HALF, HALF)], dst, sem_out.at[i])
        for i, dst in enumerate(outs)
    ]
    for copy in stores:
        copy.start()
    for copy in stores:
        copy.wait()


def attention(where, valid, stored, mine, other):
    smem = pl.BlockSpec(memory_space=pltpu.SMEM)
    vmem = pl.BlockSpec(memory_space=pltpu.VMEM)
    hbm = pl.BlockSpec(memory_space=pl.ANY)
    tiles = jax.ShapeDtypeStruct((HALF, LP, HD), BF)
    query = jax.ShapeDtypeStruct((QPD, QLEN, GROUP * HD), BF)
    own = jax.ShapeDtypeStruct((QPD, QLEN, 2 * HD), BF)
    return pl.pallas_call(
        attention_kernel,
        out_shape=(tiles,) * PARTS + (query, query, own, own),
        in_specs=[smem] * 2 + [hbm] * LOADS + [vmem] * 2,
        out_specs=(hbm,) * PARTS + (vmem,) * 4,
        scratch_shapes=[
            pltpu.VMEM((PARTS * HALF, LP, HD), BF),
            pltpu.VMEM((PARTS * HALF, LP, HD), BF),
            pltpu.SemaphoreType.DMA((LOADS * XS,)),
            pltpu.SemaphoreType.DMA((PARTS,)),
        ],
        compiler_params=pltpu.CompilerParams(vmem_limit_bytes=40 * 2**20),
        cost_estimate=pl.CostEstimate(
            flops=16 * 5 * 2 * 272 * 128 * 128, bytes_accessed=12 * 2**20, transcendentals=16 * 272 * 128
        ),
    )(where, valid, *stored, mine, other)


def total(*parts):
    out = parts[0].astype(F32)
    for part in parts[1:]:
        out = out + part.astype(F32)
    return out.astype(BF)


def per_device(
    queries,
    self_key,
    self_value,
    passage_key,
    passage_value,
    out_grad,
    block_ids,
    block_valid,
    passage_slot,
):
    core = lax.axis_index("core")
    my_zl = lax.axis_index("zl")
    swap = ring(2, 1)
    around = ("zh", "zl")
    feat = GROUP * HD

    def head(array, c, width):
        return lax.dynamic_slice_in_dim(array, c * width, width, axis=array.ndim - 1)

    def by_core(mine_part, other_part, axis):
        first = jnp.where(core == 0, mine_part, other_part)
        second = jnp.where(core == 0, other_part, mine_part)
        return jnp.concatenate([first, second], axis=axis)

    lane = lax.broadcasted_iota(jnp.int32, (1, LP, HD), 2)
    at = 4 * lax.axis_index("zh") + 2 * core
    code_tile = jnp.where(lane == at, passage_slot // 16, jnp.where(lane == at + 1, passage_slot % 16, 0))
    code_tile = code_tile.astype(BF)

    def passages(c):
        lanes = slice(c * HD, (c + 1) * HD)
        both = jnp.stack([passage_key[:, :, lanes], passage_value[:, :, lanes]], axis=1)
        return jnp.concatenate([both.reshape(TILES, LP, HD), code_tile], axis=0)

    heads = jnp.stack([passages(0), passages(1)])
    far = lax.all_to_all(
        jnp.broadcast_to(heads[None], (ZH, 2, TILES + 1, LP, HD)).reshape(2 * ZH, TILES + 1, LP, HD),
        ("zh", "core"),
        split_axis=0,
        concat_axis=0,
        tiled=True,
    )
    codes = jnp.sum(far[:, TILES:].astype(F32), axis=0).astype(BF)
    block = jnp.concatenate([far[:, :TILES].reshape(BLOCK, LP, HD), codes], axis=0)
    s0 = lax.all_to_all(
        jnp.broadcast_to(block[None], (XS, BLOCK + 1, LP, HD)),
        "x",
        split_axis=0,
        concat_axis=0,
        tiled=True,
    ).reshape(XS * (BLOCK + 1), LP, HD)

    def up(part):
        return lax.ppermute(part, around, ring(ZS, 1))

    def down(part):
        return lax.ppermute(part, around, ring(ZS, -1))

    by_x = s0.reshape(XS, BLOCK + 1, LP, HD)
    half = BLOCK // 2
    s0a = jnp.concatenate([by_x[:, :half], by_x[:, BLOCK:]], axis=1).reshape(-1, LP, HD)
    s0b = by_x[:, half:].reshape(-1, LP, HD)
    s1a, s3b = down(s0a), up(s0b)
    s2a, s2b = down(s1a), up(s3b)
    s1b, s3a = down(s0b), up(s0a)

    def pack(c):
        return jnp.concatenate(
            [
                head(queries, c, feat),
                head(out_grad, c, feat),
                head(self_key, c, HD),
                head(self_value, c, HD),
            ],
            axis=2,
        )

    mine = pack(core)
    other = lax.ppermute(pack(1 - core), "core", swap)
    lists = jnp.stack([block_ids, block_valid])
    lists_other = lax.ppermute(lists, "core", swap)

    def codes_of(part):
        return part.reshape(XS, -1, LP, HD)[:, -1, 0, :CODES]

    c0 = codes_of(s0)
    c2 = lax.ppermute(c0, around, ring(ZS, 2))
    seen = jnp.concatenate([c0, codes_of(s1a), c2, codes_of(s3b)])
    seen = seen.astype(jnp.int32).reshape(-1, 2)
    known = seen[:, 0] * 16 + seen[:, 1]
    slot_of = lax.all_to_all(
        jnp.broadcast_to(known[None], (TP,) + known.shape), "tp", split_axis=0, concat_axis=0, tiled=True
    ).reshape(-1)

    def parts(number):
        pool = number // P_DEV
        z = pool // 2 % ZS
        return pool // (2 * ZS), z // ZL, z % ZL, pool % 2, number % P_DEV

    ids = jnp.concatenate([block_ids, lists_other[0]]).reshape(-1)
    valid = jnp.concatenate([block_valid, lists_other[1]]).reshape(-1)
    x, zh, zl, c, inner = parts(ids)
    id_at = (((inner * ZL + (zl - my_zl) % ZL) * XS + x) * ZH + zh) * 2 + c
    every = jnp.arange(slot_of.shape[0], dtype=jnp.int32)
    slots = jnp.sum(jnp.where(id_at[:, None] == every[None, :], slot_of[None, :], 0), axis=1)
    x, zh, zl, c, inner = parts(slots)
    where = ((((zl - my_zl) % ZL * XS + x) * ZH + zh) * 2 + c) * TILES + 2 * inner

    *grads, dq_mine, dq_other, self_mine, self_other = attention(
        where, valid, (s0, s1a, s1b, s2a, s2b, s3a, s3b), mine, other
    )
    g0a, g0b, g1a, g1b, g2a, g2b, g3a, g3b = grads

    via_a, via_b = up(g2a), down(g2b)
    from_below_b, from_above_a = up(g1b), down(g3a)
    from_below_a = up(total(g1a, via_a))
    from_above_b = down(total(g3b, via_b))
    summed = jnp.concatenate(
        [total(g0a, from_above_a, from_below_a), total(g0b, from_below_b, from_above_b)]
    ).reshape(XS, 2 * ZH, TILES, LP, HD)
    x_parts = lax.all_to_all(summed, "x", split_axis=0, concat_axis=0, tiled=True)
    x_sum = total(*[x_parts[i] for i in range(XS)])
    far_parts = lax.all_to_all(x_sum, ("zh", "core"), split_axis=0, concat_axis=0, tiled=True)
    far_parts = far_parts.reshape(ZH, 2, P_DEV, 2, LP, HD)
    grad = total(*[far_parts[i] for i in range(ZH)])
    key_grad = jnp.concatenate([grad[0, :, 0], grad[1, :, 0]], axis=2)
    value_grad = jnp.concatenate([grad[0, :, 1], grad[1, :, 1]], axis=2)

    dq_taken = lax.ppermute(dq_other, "core", swap)
    self_taken = lax.ppermute(self_other, "core", swap)
    query_grad = by_core(dq_mine, dq_taken, 2)
    self_key_grad = by_core(self_mine[:, :, :HD], self_taken[:, :, :HD], 2)
    self_value_grad = by_core(self_mine[:, :, HD:], self_taken[:, :, HD:], 2)
    return (query_grad, self_key_grad, self_value_grad, key_grad, value_grad)


def solution(mesh):
    fine = Mesh(mesh.devices.reshape(XS, ZH, ZL, 2, TP), ("x", "zh", "zl", "core", "tp"))
    pool = ("x", "zh", "zl", "core")
    rows = P(pool, None, "tp")
    return jax.shard_map(
        per_device,
        mesh=fine,
        in_specs=(rows,) * 6 + (P(pool, None), P(pool, None), P(pool + ("tp",))),
        out_specs=(rows,) * 5,
        check_vma=False,
    )
```

```python
import jax
import jax.numpy as jnp
from jax import lax
from jax.experimental import pallas as pl
from jax.experimental.pallas import tpu as pltpu
from jax.sharding import Mesh
from jax.sharding import PartitionSpec as P

HD = 128
GROUP = 8
QLEN = 16
LP = 16
NB = 16
QPD = 8
P_DEV = 4
XS, ZH, ZL, TP = 4, 4, 4, 4
ZS = ZH * ZL
TILES = 2 * P_DEV
BLOCK = 2 * ZH * TILES
HALF = XS // 2 * BLOCK
PARTS = 2 * ZL
CODES = 4 * ZH
LOADS = 2 * ZL - 1
SCALE = HD ** (-0.5)
SPAN = NB * LP
BF = jnp.bfloat16
F32 = jnp.float32


def ring(n, d):
    return [(i, (i + d) % n) for i in range(n)]


def dot(a, b, ca, cb):
    return lax.dot_general(a, b, (((ca,), (cb,)), ((), ())), preferred_element_type=F32)


def attention_kernel(
    where_ref,
    valid_ref,
    *refs,
):
    stored, (mine, other) = refs[:LOADS], refs[LOADS : LOADS + 2]
    outs = refs[LOADS + 2 : LOADS + 2 + PARTS]
    dq_mine, dq_other, self_mine, self_other = refs[LOADS + 2 + PARTS : LOADS + 6 + PARTS]
    store, grads, sem_in, sem_out = refs[LOADS + 6 + PARTS :]
    half = BLOCK // 2
    loads = []
    for i, src in enumerate(stored):
        size = BLOCK if i == 0 else half
        first = 0 if i == 0 else (i + 1) // 2 * XS * BLOCK + (i + 1) % 2 * half
        for x in range(XS):
            loads.append(
                pltpu.make_async_copy(
                    src.at[pl.ds(x * (size + 1), size)],
                    store.at[pl.ds(first + x * BLOCK, size)],
                    sem_in.at[i * XS + x],
                )
            )
    for copy in loads:
        copy.start()

    def clear(i, carry):
        grads[pl.ds(i * 16, 16)] = jnp.zeros((16, LP, HD), BF)
        return carry

    lax.fori_loop(0, PARTS * HALF // 16, clear, 0)
    for copy in loads:
        copy.wait()

    u = lax.broadcasted_iota(jnp.int32, (QLEN, GROUP * QLEN), 0)
    t = lax.broadcasted_iota(jnp.int32, (QLEN, GROUP * QLEN), 1) % QLEN
    causal = jnp.where(u <= t, 0.0, -1e30).astype(F32)

    def stacked(ref, b, start):
        return jnp.concatenate(
            [ref[b, :, start + g * HD : start + (g + 1) * HD] for g in range(GROUP)], axis=0
        )

    def one(b, base, pack, dq_out, self_out):
        row = (base + b) * NB
        at = [where_ref[row + j] for j in range(NB)]
        q = stacked(pack, b, 0)
        do = stacked(pack, b, GROUP * HD)
        own = 2 * GROUP * HD
        keys = jnp.concatenate([store[i] for i in at] + [pack[b, :, own : own + HD]], axis=0)
        values = jnp.concatenate(
            [store[i + 1] for i in at] + [pack[b, :, own + HD : own + 2 * HD]], axis=0
        )
        bias = jnp.concatenate(
            [
                jnp.full((LP, GROUP * QLEN), jnp.where(valid_ref[row + j] > 0, 0.0, -1e30), F32)
                for j in range(NB)
            ]
            + [causal],
            axis=0,
        )
        scores = dot(keys, q, 1, 1) * SCALE + bias
        top = jnp.max(scores, axis=0, keepdims=True)
        weights = jnp.exp(scores - top)
        probs = weights * (1.0 / jnp.sum(weights, axis=0, keepdims=True))
        low = probs.astype(BF)
        dprob = dot(values, do, 1, 1)
        delta = jnp.sum(probs * dprob, axis=0, keepdims=True)
        dscore = (probs * (dprob - delta)).astype(BF)
        dq = (dot(dscore, keys, 0, 0) * SCALE).astype(BF)
        for g in range(GROUP):
            dq_out[b, :, g * HD : (g + 1) * HD] = dq[g * QLEN : (g + 1) * QLEN]
        dk = (dot(dscore, q, 1, 0) * SCALE).astype(BF)
        dv = dot(low, do, 1, 0).astype(BF)
        self_out[b, :, :HD] = dk[SPAN:]
        self_out[b, :, HD:] = dv[SPAN:]
        for j in range(NB):
            for k, part in enumerate((dk, dv)):
                to = at[j] + k
                grads[to] = (
                    grads[to].astype(F32) + part[j * LP : (j + 1) * LP].astype(F32)
                ).astype(BF)

    def step(b, carry):
        one(b, 0, mine, dq_mine, self_mine)
        one(b, QPD, other, dq_other, self_other)
        return carry

    lax.fori_loop(0, QPD, step, 0)
    stores = [
        pltpu.make_async_copy(grads.at[pl.ds(i * HALF, HALF)], dst, sem_out.at[i])
        for i, dst in enumerate(outs)
    ]
    for copy in stores:
        copy.start()
    for copy in stores:
        copy.wait()


def attention(where, valid, stored, mine, other):
    smem = pl.BlockSpec(memory_space=pltpu.SMEM)
    vmem = pl.BlockSpec(memory_space=pltpu.VMEM)
    hbm = pl.BlockSpec(memory_space=pl.ANY)
    tiles = jax.ShapeDtypeStruct((HALF, LP, HD), BF)
    query = jax.ShapeDtypeStruct((QPD, QLEN, GROUP * HD), BF)
    own = jax.ShapeDtypeStruct((QPD, QLEN, 2 * HD), BF)
    return pl.pallas_call(
        attention_kernel,
        out_shape=(tiles,) * PARTS + (query, query, own, own),
        in_specs=[smem] * 2 + [hbm] * LOADS + [vmem] * 2,
        out_specs=(hbm,) * PARTS + (vmem,) * 4,
        scratch_shapes=[
            pltpu.VMEM((PARTS * HALF, LP, HD), BF),
            pltpu.VMEM((PARTS * HALF, LP, HD), BF),
            pltpu.SemaphoreType.DMA((LOADS * XS,)),
            pltpu.SemaphoreType.DMA((PARTS,)),
        ],
        compiler_params=pltpu.CompilerParams(vmem_limit_bytes=40 * 2**20),
        cost_estimate=pl.CostEstimate(
            flops=16 * 5 * 2 * 272 * 128 * 128, bytes_accessed=12 * 2**20, transcendentals=16 * 272 * 128
        ),
    )(where, valid, *stored, mine, other)


def heads_kernel(slot_ref, at_ref, key_ref, value_ref, out_ref):
    lane = lax.broadcasted_iota(jnp.int32, (LP, HD), 1)
    slot, at = slot_ref[0], at_ref[0]
    code = jnp.where(lane == at, slot >> 4, jnp.where(lane == at + 1, slot & 15, 0))
    code = code.astype(F32).astype(BF)
    for to in range(2 * ZH):
        lanes = slice(to % 2 * HD, (to % 2 + 1) * HD)
        for i in range(P_DEV):
            out_ref[to, 2 * i] = key_ref[i, :, lanes]
            out_ref[to, 2 * i + 1] = value_ref[i, :, lanes]
        out_ref[to, TILES] = code


def heads_of(slot, at, key, value):
    smem = pl.BlockSpec(memory_space=pltpu.SMEM)
    vmem = pl.BlockSpec(memory_space=pltpu.VMEM)
    return pl.pallas_call(
        heads_kernel,
        out_shape=jax.ShapeDtypeStruct((2 * ZH, TILES + 1, LP, HD), BF),
        in_specs=[smem, smem, vmem, vmem],
        out_specs=vmem,
    )(slot, at, key, value)


def total(*parts):
    out = parts[0].astype(F32)
    for part in parts[1:]:
        out = out + part.astype(F32)
    return out.astype(BF)


def per_device(
    queries,
    self_key,
    self_value,
    passage_key,
    passage_value,
    out_grad,
    block_ids,
    block_valid,
    passage_slot,
):
    core = lax.axis_index("core")
    my_zl = lax.axis_index("zl")
    swap = ring(2, 1)
    around = ("zh", "zl")
    feat = GROUP * HD

    def head(array, c, width):
        return lax.dynamic_slice_in_dim(array, c * width, width, axis=array.ndim - 1)

    def by_core(mine_part, other_part, axis):
        first = jnp.where(core == 0, mine_part, other_part)
        second = jnp.where(core == 0, other_part, mine_part)
        return jnp.concatenate([first, second], axis=axis)

    at = (4 * lax.axis_index("zh") + 2 * core).astype(jnp.int32).reshape(1)
    far = lax.all_to_all(
        heads_of(passage_slot, at, passage_key, passage_value),
        ("zh", "core"),
        split_axis=0,
        concat_axis=0,
        tiled=True,
    )
    codes = jnp.sum(far[:, TILES:].astype(F32), axis=0).astype(BF)
    block = jnp.concatenate([far[:, :TILES].reshape(BLOCK, LP, HD), codes], axis=0)
    s0 = lax.all_to_all(
        jnp.broadcast_to(block[None], (XS, BLOCK + 1, LP, HD)),
        "x",
        split_axis=0,
        concat_axis=0,
        tiled=True,
    ).reshape(XS * (BLOCK + 1), LP, HD)

    def up(part):
        return lax.ppermute(part, around, ring(ZS, 1))

    def down(part):
        return lax.ppermute(part, around, ring(ZS, -1))

    by_x = s0.reshape(XS, BLOCK + 1, LP, HD)
    half = BLOCK // 2
    s0a = jnp.concatenate([by_x[:, :half], by_x[:, BLOCK:]], axis=1).reshape(-1, LP, HD)
    s0b = by_x[:, half:].reshape(-1, LP, HD)
    s1a, s3b = down(s0a), up(s0b)
    s2a, s2b = down(s1a), up(s3b)
    s1b, s3a = down(s0b), up(s0a)

    def pack(c):
        return jnp.concatenate(
            [
                head(queries, c, feat),
                head(out_grad, c, feat),
                head(self_key, c, HD),
                head(self_value, c, HD),
            ],
            axis=2,
        )

    mine = pack(core)
    other = lax.ppermute(pack(1 - core), "core", swap)
    lists = jnp.stack([block_ids, block_valid])
    lists_other = lax.ppermute(lists, "core", swap)

    def codes_of(part):
        return part.reshape(XS, -1, LP, HD)[:, -1, 0, :CODES]

    c0 = codes_of(s0)
    c2 = lax.ppermute(c0, around, ring(ZS, 2))
    seen = jnp.concatenate([c0, codes_of(s1a), c2, codes_of(s3b)])
    seen = seen.astype(jnp.int32).reshape(-1, 2)
    known = seen[:, 0] * 16 + seen[:, 1]
    slot_of = lax.all_to_all(
        jnp.broadcast_to(known[None], (TP,) + known.shape), "tp", split_axis=0, concat_axis=0, tiled=True
    ).reshape(-1)

    def parts(number):
        pool = number // P_DEV
        z = pool // 2 % ZS
        return pool // (2 * ZS), z // ZL, z % ZL, pool % 2, number % P_DEV

    ids = jnp.concatenate([block_ids, lists_other[0]]).reshape(-1)
    valid = jnp.concatenate([block_valid, lists_other[1]]).reshape(-1)
    x, zh, zl, c, inner = parts(ids)
    id_at = (((inner * ZL + (zl - my_zl) % ZL) * XS + x) * ZH + zh) * 2 + c
    every = jnp.arange(slot_of.shape[0], dtype=jnp.int32)
    slots = jnp.sum(jnp.where(id_at[:, None] == every[None, :], slot_of[None, :], 0), axis=1)
    x, zh, zl, c, inner = parts(slots)
    where = ((((zl - my_zl) % ZL * XS + x) * ZH + zh) * 2 + c) * TILES + 2 * inner

    *grads, dq_mine, dq_other, self_mine, self_other = attention(
        where, valid, (s0, s1a, s1b, s2a, s2b, s3a, s3b), mine, other
    )
    g0a, g0b, g1a, g1b, g2a, g2b, g3a, g3b = grads

    via_a, via_b = up(g2a), down(g2b)
    from_below_b, from_above_a = up(g1b), down(g3a)
    from_below_a = up(total(g1a, via_a))
    from_above_b = down(total(g3b, via_b))
    summed = jnp.concatenate(
        [total(g0a, from_above_a, from_below_a), total(g0b, from_below_b, from_above_b)]
    ).reshape(XS, 2 * ZH, TILES, LP, HD)
    x_parts = lax.all_to_all(summed, "x", split_axis=0, concat_axis=0, tiled=True)
    x_sum = total(*[x_parts[i] for i in range(XS)])
    far_parts = lax.all_to_all(x_sum, ("zh", "core"), split_axis=0, concat_axis=0, tiled=True)
    far_parts = far_parts.reshape(ZH, 2, P_DEV, 2, LP, HD)
    grad = total(*[far_parts[i] for i in range(ZH)])
    key_grad = jnp.concatenate([grad[0, :, 0], grad[1, :, 0]], axis=2)
    value_grad = jnp.concatenate([grad[0, :, 1], grad[1, :, 1]], axis=2)

    dq_taken = lax.ppermute(dq_other, "core", swap)
    self_taken = lax.ppermute(self_other, "core", swap)
    query_grad = by_core(dq_mine, dq_taken, 2)
    self_key_grad = by_core(self_mine[:, :, :HD], self_taken[:, :, :HD], 2)
    self_value_grad = by_core(self_mine[:, :, HD:], self_taken[:, :, HD:], 2)
    return (query_grad, self_key_grad, self_value_grad, key_grad, value_grad)


def solution(mesh):
    fine = Mesh(mesh.devices.reshape(XS, ZH, ZL, 2, TP), ("x", "zh", "zl", "core", "tp"))
    pool = ("x", "zh", "zl", "core")
    rows = P(pool, None, "tp")
    return jax.shard_map(
        per_device,
        mesh=fine,
        in_specs=(rows,) * 6 + (P(pool, None), P(pool, None), P(pool + ("tp",))),
        out_specs=(rows,) * 5,
        check_vma=False,
    )
```
